128 devices in a mesh: dp: 4 (over y_hi, core), ctx: 32 (over y_lo, z, x).
Axes of the slice: x: 4, y: 4 (y_hi: 2, y_lo: 2; y = y_hi * 2 + y_lo), z: 4, core: 2. Of those that a mesh axis runs over, the one named last changes fastest.
Arguments:
- gate_values: bfloat16 [4, 4096, 4096], P('dp', 'ctx'), may hold values from -6 to 6
- conv_input: bfloat16 [4, 4096, 4096], P('dp', 'ctx'), may hold values from -6 to 6
- cotangent: bfloat16 [4, 4096, 4096], P('dp', 'ctx'), may hold values from -6 to 6
- filters: bfloat16 [256, 4096], P('ctx'), may hold values from -1.4 to 1.4
- direct_scale: float32 [4096], P('ctx'), may hold values from -1 to 1
Outputs:
- gate_grad: bfloat16 [4, 4096, 4096], P('dp', 'ctx')
- input_grad: bfloat16 [4, 4096, 4096], P('dp', 'ctx')
- filter_grad: float32 [256, 4096], P('ctx', 'dp')
The draws below stay inside these ranges and needn't reach their ends.
All inputs are finite; a program needn't handle non-finite values.
Results may differ from the reference program's by a relative error of at most 0.012.
Values may be sent and summed in bfloat16 or wider, within the bound.
No kernel may reach another device: no remote copies, remote signals or barrier semaphores. Data moves between devices by JAX's collectives and lax.ppermute only.
A program may use at most 128 MiB of HBM per device.

```python
import math
import jax
import jax.numpy as jnp
from jax import lax

CHANNELS = 4096
GROUP_WIDTH = 16
SECTION_B = 128
TIME_STEP_COUNT = 4096
NFFT = 8192
SECTION_A = 64
BATCH = 4
KERNEL_FAMILIES = 256


def draw_filters(key, part):
    key = jax.random.fold_in(key, 11)
    stochastic_seeds = jax.random.split(key, 5)
    slow_share = 0.5
    rough = jax.random.truncated_normal(stochastic_seeds[0], -4.0, 4.0, (KERNEL_FAMILIES, TIME_STEP_COUNT), jnp.float32)
    slow_pick = jax.random.uniform(stochastic_seeds[1], (KERNEL_FAMILIES, 1), jnp.float32) < slow_share
    fast_tau = jnp.exp(jax.random.uniform(stochastic_seeds[2], (KERNEL_FAMILIES, 1), jnp.float32, math.log(16.0), math.log(48.0)))
    slow_tau = jnp.exp(jax.random.uniform(stochastic_seeds[3], (KERNEL_FAMILIES, 1), jnp.float32, math.log(TIME_STEP_COUNT / 2.0), math.log(8.0 * TIME_STEP_COUNT)))
    decay_len = jnp.where(slow_pick, slow_tau, fast_tau)
    time_slot_number = jnp.arange(TIME_STEP_COUNT, dtype=jnp.int32)
    packet_portions = jax.random.randint(stochastic_seeds[4], (KERNEL_FAMILIES, 3, 1), 1, TIME_STEP_COUNT)
    forwarded_quantities = jnp.sum((time_slot_number[None, None, :] >= packet_portions).astype(jnp.float32), axis=1)
    amplitude = jnp.sqrt(1.0 - jnp.exp(-2.0 / decay_len))
    envelope = jnp.exp(-time_slot_number.astype(jnp.float32)[None, :] / decay_len) * jnp.power(0.6, forwarded_quantities)
    return (rough * amplitude * envelope).astype(jnp.bfloat16)


def level_of(key, shape, cuts, smallest, largest):
    def one(dim, parts):
        steps = jax.random.uniform(jax.random.fold_in(jax.random.fold_in(key, 6), dim), (parts,), jnp.float32, smallest / len(cuts), largest / len(cuts))
        return jnp.repeat(jnp.exp(steps), shape[dim] // parts).reshape((-1,) + (1,) * (len(shape) - dim - 1))

    gain = one(*cuts[0])
    for cut in cuts[1:]:
        gain = gain * one(*cut)
    return gain


def gaussian(stream_key, dims, scale, bound, cuts=(), held_as=jnp.bfloat16):
    entries = scale * jax.random.normal(stream_key, dims, jnp.float32)
    if cuts:
        entries = entries * level_of(stream_key, dims, cuts, -0.22, 0.18)
    return jnp.clip(entries, -bound, bound).astype(held_as)


def setup_inputs(seed: int = 0) -> dict:
    key_list = jax.random.split(jax.random.key(seed), 6)
    gate_values = gaussian(key_list[0], (BATCH, TIME_STEP_COUNT, CHANNELS), 1.0, 6.0, ((0, 4), (1, 32)))
    conv_input = gaussian(key_list[1], (BATCH, TIME_STEP_COUNT, CHANNELS), 1.0, 6.0, ((0, 4), (1, 32)))
    cotangent = gaussian(key_list[2], (BATCH, TIME_STEP_COUNT, CHANNELS), 1.0, 6.0, ((0, 4), (1, 32)))
    filters = draw_filters(jax.random.fold_in(key_list[5], 71), 0)
    direct_scale = jnp.clip(jax.random.uniform(key_list[4], (CHANNELS,), jnp.float32, -1.0, 1.0) * level_of(key_list[4], (CHANNELS,), ((0, 32),), -0.4, 0.0), -1.0, 1.0)
    return dict(gate_values=gate_values, conv_input=conv_input, cotangent=cotangent, filters=filters, direct_scale=direct_scale)


def angle_tables(row_count, column_count, modulus):
    left_index = jnp.arange(row_count, dtype=jnp.int32)[:, None]
    right_index = jnp.arange(column_count, dtype=jnp.int32)[None, :]
    phase_angle = (left_index * right_index % modulus).astype(jnp.float32) * (2.0 * math.pi / modulus)
    return (jnp.cos(phase_angle), jnp.sin(phase_angle))

def rounded(values):
    return lax.optimization_barrier(values.astype(jnp.bfloat16)).astype(jnp.float32)

def contract(form, left_side, right_side):
    return jnp.einsum(form, left_side, right_side, precision=lax.Precision.HIGHEST)

def spectrum(signal):
    cos_one, sin_one = angle_tables(SECTION_A, SECTION_A // 2, SECTION_A)
    cos_one, sin_one = (rounded(cos_one), rounded(sin_one))
    turn_cos, turn_sin = angle_tables(SECTION_A, SECTION_B, NFFT)
    cos_two, sin_two = angle_tables(SECTION_B, SECTION_B, SECTION_B)
    cos_two, sin_two = (rounded(cos_two), rounded(sin_two))
    signal_grid = signal.astype(jnp.float32).reshape(-1, SECTION_A // 2, SECTION_B)
    first_real = contract('kn,cnm->ckm', cos_one, signal_grid)
    first_imag = -contract('kn,cnm->ckm', sin_one, signal_grid)
    turned_real = rounded(first_real * turn_cos + first_imag * turn_sin)
    turned_imag = rounded(first_imag * turn_cos - first_real * turn_sin)
    spec_real = contract('ckm,mj->ckj', turned_real, cos_two) + contract('ckm,mj->ckj', turned_imag, sin_two)
    spec_imag = contract('ckm,mj->ckj', turned_imag, cos_two) - contract('ckm,mj->ckj', turned_real, sin_two)
    return (spec_real, spec_imag)

def restore(part_real, part_imag):
    cos_one, sin_one = angle_tables(SECTION_A, SECTION_A // 2, SECTION_A)
    cos_one, sin_one = (rounded(cos_one), rounded(sin_one))
    turn_cos, turn_sin = angle_tables(SECTION_A, SECTION_B, NFFT)
    cos_two, sin_two = angle_tables(SECTION_B, SECTION_B, SECTION_B)
    cos_two, sin_two = (rounded(cos_two), rounded(sin_two))
    back_real = contract('ckm,mj->ckj', part_real, cos_two) - contract('ckm,mj->ckj', part_imag, sin_two)
    back_imag = contract('ckm,mj->ckj', part_real, sin_two) + contract('ckm,mj->ckj', part_imag, cos_two)
    turned_real = rounded(back_real * turn_cos - back_imag * turn_sin)
    turned_imag = rounded(back_real * turn_sin + back_imag * turn_cos)
    result = contract('kn,ckm->cnm', cos_one, turned_real) - contract('kn,ckm->cnm', sin_one, turned_imag)
    return result.reshape(result.shape[0], TIME_STEP_COUNT)

def reference(gate_values, conv_input, cotangent, filters, direct_scale):
    grad_scale = 1.0 / (NFFT * math.sqrt(GROUP_WIDTH * BATCH * TIME_STEP_COUNT))

    def group_terms(group_index):
        offset = group_index * GROUP_WIDTH
        inputs = lax.dynamic_slice_in_dim(conv_input, offset, GROUP_WIDTH, 2)
        gates = lax.dynamic_slice_in_dim(gate_values, offset, GROUP_WIDTH, 2)
        cotan = lax.dynamic_slice_in_dim(cotangent, offset, GROUP_WIDTH, 2)
        skip_part = lax.dynamic_slice_in_dim(direct_scale, offset, GROUP_WIDTH, 0)
        kernel = lax.dynamic_slice_in_dim(filters, group_index, 1, 0)
        grad_local = (cotan.astype(jnp.float32) * gates.astype(jnp.float32)).astype(jnp.bfloat16)
        input_rows = jnp.transpose(inputs, (0, 2, 1)).reshape(-1, TIME_STEP_COUNT)
        grad_rows = jnp.transpose(grad_local, (0, 2, 1)).reshape(-1, TIME_STEP_COUNT)
        cotan_rows = jnp.transpose(cotan, (0, 2, 1)).reshape(-1, TIME_STEP_COUNT)
        gain_rows = jnp.tile(skip_part, BATCH)[:, None]
        in_real, in_imag = spectrum(input_rows)
        gradient_real, gr_imag = spectrum(grad_rows)
        ke_real, ke_imag = spectrum(kernel)
        smoothed_lines = restore(rounded(ke_real * in_real - ke_imag * in_imag), rounded(ke_real * in_imag + ke_imag * in_real)) * (1.0 / NFFT)
        mixed_rows = (smoothed_lines + gain_rows * input_rows.astype(jnp.float32)).astype(jnp.bfloat16)
        adjoint_rows = restore(rounded(ke_real * gradient_real + ke_imag * gr_imag), rounded(ke_real * gr_imag - ke_imag * gradient_real)) * (1.0 / NFFT)
        in_grad = (adjoint_rows + gain_rows * grad_rows.astype(jnp.float32)).astype(jnp.bfloat16)
        gate_rows = (cotan_rows.astype(jnp.float32) * mixed_rows.astype(jnp.float32)).astype(jnp.bfloat16)
        spec_real = lax.optimization_barrier(jnp.sum(in_real * gradient_real + in_imag * gr_imag, axis=0))
        spec_imag = lax.optimization_barrier(jnp.sum(in_real * gr_imag - in_imag * gradient_real, axis=0))
        filter_rows = restore(rounded(spec_real)[None], rounded(spec_imag)[None])[0] * grad_scale
        return (gate_rows.reshape(BATCH, GROUP_WIDTH, TIME_STEP_COUNT), in_grad.reshape(BATCH, GROUP_WIDTH, TIME_STEP_COUNT), filter_rows)
    gate_all, input_all, filter_grad = lax.map(group_terms, jnp.arange(KERNEL_FAMILIES, dtype=jnp.int32))
    gate_grad = jnp.transpose(gate_all, (1, 3, 0, 2)).reshape(BATCH, TIME_STEP_COUNT, CHANNELS)
    input_grad = jnp.transpose(input_all, (1, 3, 0, 2)).reshape(BATCH, TIME_STEP_COUNT, CHANNELS)
    return (gate_grad, input_grad, filter_grad)
```

```python
import math

import jax
import jax.numpy as jnp
import numpy as np
from jax import lax
from jax.experimental import pallas as pl
from jax.experimental.pallas import tpu as pltpu
from jax.sharding import PartitionSpec as P

GROUP_WIDTH = 16
OUTER = 32
INNER = 128
POINTS = 8192
LANES = 128
F32 = jnp.float32
BF16 = jnp.bfloat16


def turns(numerator, denominator):
    angle = 2.0 * np.pi * (np.asarray(numerator) % denominator) / denominator
    return np.cos(angle), np.sin(angle)


def build_tables(grad_scale):
    eye = np.eye(8)
    slab = np.arange(OUTER)[:, None, None]
    outer = np.arange(OUTER)[None, :, None]
    step = np.arange(8)[None, None, :]
    cos_part, sin_part = turns(slab * (128 * outer + step), POINTS)
    first = np.concatenate([cos_part, -sin_part], 0)
    first[0] = 1.0
    first[OUTER] = (1.0 - 2.0 * (np.arange(OUTER) % 2))[:, None]
    table_one = np.einsum("rns,st->rtns", first, eye).reshape(512, 256)
    table_last = table_one.T * (2.0 / POINTS)

    index = np.arange(INNER)
    cos_two, sin_two = turns(index[:, None] * index[None, :], INNER)
    table_two = np.block([[cos_two, sin_two], [-sin_two, cos_two]])
    half = np.arange(64)
    cos_low, sin_low = turns(half[:, None] * index[None, :], INNER)
    cos_mid, sin_mid = turns((32 + 64 * half[:, None]) * index[None, :], POINTS)
    zero = np.zeros((64, INNER))
    sin_low = -sin_low
    sin_low[0] = 1.0 - 2.0 * (index % 2)
    table_two_zero = np.block(
        [[cos_low, zero], [zero, cos_mid], [sin_low, zero], [zero, -sin_mid]]
    )
    weight = np.ones((256, 1))
    weight[0] = 0.5
    weight[128] = 0.5
    table_three = table_two.T
    table_three_zero = (table_two_zero * weight).T

    cos_q, sin_q = turns(np.arange(OUTER)[:, None] * 8 * np.arange(16)[None, :], POINTS)
    scalars = np.concatenate([cos_q.reshape(-1), sin_q.reshape(-1)])

    member = np.zeros((8, 256, LANES))
    for pair in range(8):
        for side in range(2):
            for channel in range(LANES):
                lane = (2 * pair + side) * 8 + channel // GROUP_WIDTH
                member[pair, side * LANES + channel, lane] = 1.0
    slab_lane = np.repeat(np.arange(OUTER), 8)
    group_lane = np.tile(np.arange(8), OUTER)
    turn_cos, turn_sin = turns(index[:, None] * slab_lane[None, :], POINTS)
    last_cos, last_sin = turns(slab_lane[:, None] * np.arange(OUTER)[None, :], 64)
    last_sin = -last_sin
    last_sin[slab_lane == 0] = 1.0 - 2.0 * (np.arange(OUTER) % 2)
    parts = np.stack([last_cos, last_sin])
    same = group_lane[:, None] == np.arange(8)[None, :]
    table_grad = np.einsum("pln,lg->plgn", parts, same)
    table_grad = table_grad.reshape(2, 256, 8, 4, 8).transpose(0, 1, 3, 2, 4)
    table_grad = table_grad.reshape(512, 256) * (2.0 * grad_scale)

    def low(values):
        return jnp.asarray(values, BF16)

    def wide(values):
        return jnp.asarray(values, F32)

    return dict(
        one=low(table_one),
        last=low(table_last),
        two=low(table_two),
        two_zero=low(table_two_zero),
        three=low(table_three),
        three_zero=low(table_three_zero),
        scalars=wide(scalars),
        member=low(member),
        turn_cos=wide(turn_cos),
        turn_sin=wide(turn_sin),
        grad=low(table_grad),
    )


def dot(left, right):
    return jnp.dot(left, right, preferred_element_type=F32)


def halves(values):
    values = values.astype(F32)
    rows = values.shape[0] * 8
    return jnp.concatenate(
        [values[:, :8].reshape(rows, LANES), values[:, 8:].reshape(rows, LANES)], 1
    )


def outer_stage(v_ref, one_ref, w_ref, u_ref):
    @pl.loop(0, 8)
    def _(p):
        row = pl.multiple_of(p * 16, 16)
        first = dot(one_ref[...], halves(v_ref[:, pl.ds(row, 16), :]).astype(BF16))
        for j in range(OUTER):
            real, imag = [], []
            for h in range(2):
                c = w_ref[j * 16 + 2 * p + h]
                s = w_ref[512 + j * 16 + 2 * p + h]
                fr = first[8 * j : 8 * j + 8, LANES * h : LANES * h + LANES]
                fi = first[256 + 8 * j : 264 + 8 * j, LANES * h : LANES * h + LANES]
                real.append(fr * c + fi * s)
                imag.append(fi * c - fr * s)
            u_ref[j, pl.ds(row, 16), :] = jnp.concatenate(real, 0).astype(BF16)
            u_ref[OUTER + j, pl.ds(row, 16), :] = jnp.concatenate(imag, 0).astype(BF16)


def load_pair(u_ref, j):
    return jnp.concatenate(
        [
            jnp.concatenate([u_ref[j], u_ref[j + 1]], 1),
            jnp.concatenate([u_ref[OUTER + j], u_ref[OUTER + j + 1]], 1),
        ],
        0,
    )


def load_one(u_ref, j):
    return jnp.concatenate([u_ref[j], u_ref[OUTER + j]], 0)


def load_spec(ref, j, count):
    if count == 1:
        return ref[j].astype(F32), ref[OUTER + j].astype(F32)
    return (
        jnp.concatenate([ref[j], ref[j + 1]], 1).astype(F32),
        jnp.concatenate([ref[OUTER + j], ref[OUTER + j + 1]], 1).astype(F32),
    )


def store_spec(ref, j, count, real, imag):
    for h in range(count):
        ref[j + h] = real[:, LANES * h : LANES * h + LANES].astype(ref.dtype)
        ref[OUTER + j + h] = imag[:, LANES * h : LANES * h + LANES].astype(ref.dtype)


def times(ar, ai, br, bi, conjugate, packed):
    cross = ai * bi
    if conjugate:
        real, imag = ar * br + cross, ar * bi - ai * br
    else:
        real, imag = ar * br - cross, ar * bi + ai * br
    if packed:
        edge = lax.broadcasted_iota(jnp.int32, ar.shape, 0) == 0
        real = jnp.where(edge, ar * br, real)
        imag = jnp.where(edge, cross, imag)
    return real, imag


def turn_back(u_ref, w_ref, j, count, back):
    for h in range(count):
        for q in range(0, 16, 2):
            real, imag = [], []
            for k in (q, q + 1):
                c = w_ref[(j + h) * 16 + k]
                s = w_ref[512 + (j + h) * 16 + k]
                br = back[8 * k : 8 * k + 8, LANES * h : LANES * h + LANES]
                bi = back[128 + 8 * k : 136 + 8 * k, LANES * h : LANES * h + LANES]
                real.append(br * c - bi * s)
                imag.append(br * s + bi * c)
            u_ref[j + h, 8 * q : 8 * q + 16, :] = jnp.concatenate(real, 0).astype(BF16)
            u_ref[OUTER + j + h, 8 * q : 8 * q + 16, :] = jnp.concatenate(imag, 0).astype(BF16)


def last_stage(u_ref, v_ref, gain_ref, last_ref, out_ref):
    @pl.loop(0, 8)
    def _(p):
        row = pl.multiple_of(p * 16, 16)
        lines = dot(last_ref[...], halves(u_ref[:, pl.ds(row, 16), :]).astype(BF16))
        gain = gain_ref[...]
        given = v_ref[:, pl.ds(row, 16), :].astype(F32)
        low = lines[:, :LANES].reshape(OUTER, 8, LANES) + gain * given[:, :8]
        high = lines[:, LANES:].reshape(OUTER, 8, LANES) + gain * given[:, 8:]
        out_ref[:, pl.ds(row, 16), :] = jnp.concatenate([low, high], 1).astype(BF16)


def slabs(body):
    body(0, 1, True)
    body(1, 1, False)

    @pl.loop(1, OUTER // 2)
    def _(m):
        body(2 * m, 2, False)


def filter_kernel(w_ref, v_ref, one_ref, two_ref, two_zero_ref, spec_ref, u_ref):
    outer_stage(v_ref, one_ref, w_ref, u_ref)

    def body(j, count, packed):
        held = load_one(u_ref, j) if count == 1 else load_pair(u_ref, j)
        spec = dot((two_zero_ref if packed else two_ref)[...], held)
        store_spec(spec_ref, j, count, spec[:128], spec[128:])

    slabs(body)


def input_kernel(
    w_ref, v_ref, h_ref, gain_ref, one_ref, two_ref, two_zero_ref, three_ref, three_zero_ref,
    last_ref, out_ref, spec_ref, u_ref,
):
    outer_stage(v_ref, one_ref, w_ref, u_ref)

    def body(j, count, packed):
        held = load_one(u_ref, j) if count == 1 else load_pair(u_ref, j)
        spec = dot((two_zero_ref if packed else two_ref)[...], held)
        xr, xi = spec[:128], spec[128:]
        store_spec(spec_ref, j, count, xr, xi)
        hr, hi = load_spec(h_ref, j, count)
        pr, pi = times(hr, hi, xr, xi, False, packed)
        product = jnp.concatenate([pr, pi], 0).astype(BF16)
        back = dot((three_zero_ref if packed else three_ref)[...], product)
        turn_back(u_ref, w_ref, j, count, back)

    slabs(body)
    last_stage(u_ref, v_ref, gain_ref, last_ref, out_ref)


def gradient_kernel(
    w_ref, v_ref, h_ref, x_ref, gain_ref, one_ref, two_ref, two_zero_ref, three_ref,
    three_zero_ref, last_ref, member_ref, turn_cos_ref, turn_sin_ref, grad_ref,
    out_ref, filter_ref, u_ref, sum_ref,
):
    outer_stage(v_ref, one_ref, w_ref, u_ref)
    sum_ref[...] = jnp.zeros_like(sum_ref)

    def body(j, count, packed):
        held = load_one(u_ref, j) if count == 1 else load_pair(u_ref, j)
        spec = dot((two_zero_ref if packed else two_ref)[...], held)
        gr, gi = spec[:128], spec[128:]
        hr, hi = load_spec(h_ref, j, count)
        pr, pi = times(hr, hi, gr, gi, True, packed)
        product = jnp.concatenate([pr, pi], 0).astype(BF16)
        back = dot((three_zero_ref if packed else three_ref)[...], product)
        turn_back(u_ref, w_ref, j, count, back)
        xr, xi = load_spec(x_ref, j, count)
        fr, fi = times(xr, xi, gr, gi, True, packed)
        both = jnp.concatenate([fr, fi], 0)
        high = both.astype(BF16)
        rest = (both - high.astype(F32)).astype(BF16)
        pair = (j // 2) % 8
        if count == 1:
            member = member_ref[pair, pl.ds(LANES * j, LANES), :]
        else:
            member = member_ref[pair]
        sum_ref[j // 16] += dot(high, member) + dot(rest, member)

    slabs(body)
    last_stage(u_ref, v_ref, gain_ref, last_ref, out_ref)

    total = jnp.concatenate([sum_ref[0], sum_ref[1]], 1).astype(BF16)
    back = dot(three_ref[...], total)
    back_zero = dot(three_zero_ref[...], total)
    packed = lax.broadcasted_iota(jnp.int32, back.shape, 1) < 8
    back = jnp.where(packed, back_zero, back)
    br, bi = back[:128], back[128:]
    c, s = turn_cos_ref[...], turn_sin_ref[...]
    turned = jnp.concatenate([br * c - bi * s, br * s + bi * c], 1).astype(BF16)
    filter_ref[...] = dot(turned, grad_ref[...]).T


SMEM_SPEC = pl.BlockSpec(memory_space=pltpu.SMEM)
VMEM_SPEC = pl.BlockSpec(memory_space=pltpu.VMEM)
PARAMS = pltpu.CompilerParams(vmem_limit_bytes=48 * 1024 * 1024)
BLOCK = jax.ShapeDtypeStruct((OUTER, INNER, LANES), BF16)
SPEC = jax.ShapeDtypeStruct((2 * OUTER, INNER, LANES), F32)
HELD = pltpu.VMEM((2 * OUTER, INNER, LANES), BF16)


def call(kernel, operands, outs, scratch, flops):
    return pl.pallas_call(
        kernel,
        out_shape=outs,
        in_specs=[SMEM_SPEC] + [VMEM_SPEC] * (len(operands) - 1),
        out_specs=jax.tree.map(lambda _: VMEM_SPEC, outs),
        scratch_shapes=scratch,
        compiler_params=PARAMS,
        cost_estimate=pl.CostEstimate(flops=flops, bytes_accessed=16 << 20, transcendentals=0),
    )(*operands)


def filter_spectrum(tables, spread):
    t = tables
    return call(
        filter_kernel,
        (t["scalars"], spread, t["one"], t["two"], t["two_zero"]),
        SPEC, [HELD], 2 << 30,
    )


def input_path(tables, moved, kernel_spec, gains):
    t = tables
    return call(
        input_kernel,
        (t["scalars"], moved, kernel_spec, gains, t["one"], t["two"], t["two_zero"],
         t["three"], t["three_zero"], t["last"]),
        (BLOCK, SPEC), [HELD], 4 << 30,
    )


def gradient_path(tables, moved, kernel_spec, input_spec, gains):
    t = tables
    return call(
        gradient_kernel,
        (t["scalars"], moved, kernel_spec, input_spec, gains, t["one"], t["two"], t["two_zero"],
         t["three"], t["three_zero"], t["last"], t["member"], t["turn_cos"], t["turn_sin"],
         t["grad"]),
        (BLOCK, jax.ShapeDtypeStruct((256, LANES), F32)),
        [HELD, pltpu.VMEM((2, 256, LANES), F32)],
        6 << 30,
    )


def spread_filters(filters):
    groups = filters.shape[0]
    member = np.repeat(np.eye(groups), LANES // groups, axis=1)
    return jnp.einsum(
        "gt,gc->tc", filters, jnp.asarray(member, BF16), preferred_element_type=F32
    ).astype(BF16).reshape(OUTER, INNER, LANES)


def exchange(blocks):
    return lax.all_to_all(blocks, "ctx", split_axis=0, concat_axis=0, tiled=True)


def by_channel(rows):
    return jnp.transpose(rows.reshape(INNER, OUTER, LANES), (1, 0, 2))


def by_position(blocks):
    return jnp.transpose(blocks, (1, 0, 2)).reshape(INNER, OUTER * LANES)


def on_device(gate_values, conv_input, cotangent, filters, direct_scale):
    replica_count = lax.axis_size("dp")
    grad_scale = 1.0 / (POINTS * math.sqrt(GROUP_WIDTH * replica_count * POINTS // 2))
    tables = build_tables(grad_scale)
    gains = direct_scale[None, :]
    moved_input = exchange(by_channel(conv_input[0]))
    gated = (cotangent[0].astype(F32) * gate_values[0].astype(F32)).astype(BF16)
    moved_grad = exchange(by_channel(gated))
    kernel_spec = filter_spectrum(tables, spread_filters(filters))
    mixed, input_spec = input_path(tables, moved_input, kernel_spec, gains)
    back_mixed = exchange(mixed)
    in_grad, filter_part = gradient_path(tables, moved_grad, kernel_spec, input_spec, gains)
    back_input = exchange(in_grad)
    filter_grad = lax.psum_scatter(
        filter_part.reshape(replica_count, -1, LANES), "dp", scatter_dimension=0, tiled=True
    ).reshape(filters.shape[0], -1)
    gate_grad = (cotangent[0].astype(F32) * by_position(back_mixed).astype(F32)).astype(BF16)
    return gate_grad[None], by_position(back_input)[None], filter_grad


def solution(mesh):
    placed = (
        P("dp", "ctx", None),
        P("dp", "ctx", None),
        P("dp", "ctx", None),
        P("ctx", None),
        P("ctx"),
    )
    return jax.shard_map(
        on_device,
        mesh=mesh,
        in_specs=placed,
        out_specs=(P("dp", "ctx", None), P("dp", "ctx", None), P("ctx", "dp")),
        check_vma=False,
    )
```

```python
import math

import jax
import jax.numpy as jnp
import numpy as np
from jax import lax
from jax.experimental import pallas as pl
from jax.experimental.pallas import tpu as pltpu
from jax.sharding import PartitionSpec as P

GROUP_WIDTH = 16
OUTER = 32
INNER = 128
POINTS = 8192
LANES = 128
PAIR = 2 * LANES
F32 = jnp.float32
BF16 = jnp.bfloat16


def turns(numerator, denominator):
    angle = 2.0 * np.pi * (np.asarray(numerator) % denominator) / denominator
    return np.cos(angle), np.sin(angle)


def build_tables(grad_scale):
    eye = np.eye(8)
    slab = np.arange(OUTER)[:, None, None]
    outer = np.arange(OUTER)[None, :, None]
    step = np.arange(INNER)[None, None, :]
    cos_part, sin_part = turns(slab * (128 * outer + step), POINTS)
    first = np.concatenate([cos_part, -sin_part], 0)
    first[0] = 1.0
    first[OUTER] = (1.0 - 2.0 * (np.arange(OUTER) % 2))[:, None]
    table_one = np.einsum("rnqs,st->qrtns", first.reshape(64, OUTER, 16, 8), eye)
    table_one = table_one.reshape(16, 512, 256)
    table_last = table_one.transpose(0, 2, 1) * (2.0 / POINTS)

    index = np.arange(INNER)
    cos_two, sin_two = turns(index[:, None] * index[None, :], INNER)
    table_two = np.block([[cos_two, sin_two], [-sin_two, cos_two]])
    half = np.arange(64)
    cos_low, sin_low = turns(half[:, None] * index[None, :], INNER)
    cos_mid, sin_mid = turns((32 + 64 * half[:, None]) * index[None, :], POINTS)
    zero = np.zeros((64, INNER))
    sin_low = -sin_low
    sin_low[0] = 1.0 - 2.0 * (index % 2)
    table_two_zero = np.block(
        [[cos_low, zero], [zero, cos_mid], [sin_low, zero], [zero, -sin_mid]]
    )
    weight = np.ones((256, 1))
    weight[0] = 0.5
    weight[128] = 0.5
    table_three = table_two.T
    table_three_zero = (table_two_zero * weight).T

    member = np.zeros((8, 256, LANES))
    for pair in range(8):
        for side in range(2):
            for channel in range(LANES):
                lane = (2 * pair + side) * 8 + channel // GROUP_WIDTH
                member[pair, side * LANES + channel, lane] = 1.0
    slab_lane = np.repeat(np.arange(OUTER), 8)
    group_lane = np.tile(np.arange(8), OUTER)
    turn_cos, turn_sin = turns(index[:, None] * slab_lane[None, :], POINTS)
    last_cos, last_sin = turns(slab_lane[:, None] * np.arange(OUTER)[None, :], 64)
    last_sin = -last_sin
    last_sin[slab_lane == 0] = 1.0 - 2.0 * (np.arange(OUTER) % 2)
    parts = np.stack([last_cos, last_sin])
    same = group_lane[:, None] == np.arange(8)[None, :]
    table_grad = np.einsum("pln,lg->plgn", parts, same)
    table_grad = table_grad.reshape(2, 256, 8, 4, 8).transpose(0, 1, 3, 2, 4)
    table_grad = table_grad.reshape(512, 256) * (2.0 * grad_scale)

    def low(values):
        return jnp.asarray(values, BF16)

    def wide(values):
        return jnp.asarray(values, F32)

    return dict(
        one=low(table_one),
        last=low(table_last),
        two=low(table_two),
        two_zero=low(table_two_zero),
        three=low(table_three),
        three_zero=low(table_three_zero),
        member=low(member),
        turn_cos=wide(turn_cos),
        turn_sin=wide(turn_sin),
        grad=low(table_grad),
    )


def dot(left, right):
    return jnp.dot(left, right, preferred_element_type=F32)


def outer_stage(load, one_ref, u_ref):
    @pl.loop(0, 8)
    def _(p):
        row = pl.multiple_of(p * 16, 16)
        given = load(row)
        lanes = given.shape[2]
        out = []
        for h in range(2):
            held = given[:, 8 * h : 8 * h + 8].reshape(256, lanes).astype(BF16)
            out.append(dot(one_ref[2 * p + h], held).reshape(64, 8, lanes))
        u_ref[:, pl.ds(row, 16), :] = jnp.concatenate(out, 1).astype(BF16)


def slab_matrix(u_ref, start, count):
    real = [u_ref[start + k] for k in range(count)]
    imag = [u_ref[OUTER + start + k] for k in range(count)]
    return jnp.concatenate([jnp.concatenate(real, 1), jnp.concatenate(imag, 1)], 0)


def times(ar, ai, br, bi, conjugate, packed):
    cross = ai * bi
    if conjugate:
        real, imag = ar * br + cross, ar * bi - ai * br
    else:
        real, imag = ar * br - cross, ar * bi + ai * br
    if packed:
        edge = lax.broadcasted_iota(jnp.int32, ar.shape, 0) == 0
        real = jnp.where(edge, ar * br, real)
        imag = jnp.where(edge, cross, imag)
    return real, imag


def slabs(body, count):
    body(0, 1, True)
    body(1, count - 1, False)

    @pl.loop(1, OUTER // count)
    def _(m):
        body(count * m, count, False)


def filter_kernel(v_ref, one_ref, two_ref, two_zero_ref, spec_ref, u_ref):
    outer_stage(lambda row: v_ref[:, pl.ds(row, 16), :].astype(F32), one_ref, u_ref)

    def body(start, count, packed):
        spec = dot((two_zero_ref if packed else two_ref)[...], slab_matrix(u_ref, start, count))
        for k in range(count):
            spec_ref[start + k] = spec[:INNER, LANES * k : LANES * k + LANES]
            spec_ref[OUTER + start + k] = spec[INNER:, LANES * k : LANES * k + LANES]

    slabs(body, 4)


def main_kernel(
    v_ref, h_ref, gain_ref, one_ref, two_ref, two_zero_ref, three_ref, three_zero_ref, last_ref,
    out_ref, u_ref, back_ref,
):
    def load(row):
        both = v_ref[:, :, pl.ds(row, 16), :].astype(F32)
        return jnp.concatenate([both[:, 0], both[:, 1]], 2)

    outer_stage(load, one_ref, u_ref)

    def body(start, count, packed):
        spec = dot((two_zero_ref if packed else two_ref)[...], slab_matrix(u_ref, start, count))
        top, bottom = [], []
        for k in range(count):
            real = spec[:INNER, PAIR * k : PAIR * k + PAIR]
            imag = spec[INNER:, PAIR * k : PAIR * k + PAIR]
            hr, hi = h_ref[start + k], h_ref[OUTER + start + k]
            pr, pi = times(hr, hi, real[:, :LANES], imag[:, :LANES], False, packed)
            ar, ai = times(hr, hi, real[:, LANES:], imag[:, LANES:], True, packed)
            top += [pr, ar]
            bottom += [pi, ai]
        product = jnp.concatenate(
            [jnp.concatenate(top, 1), jnp.concatenate(bottom, 1)], 0
        ).astype(BF16)
        back = dot((three_zero_ref if packed else three_ref)[...], product)
        for k in range(count):
            u_ref[start + k] = spec[:INNER, PAIR * k : PAIR * k + PAIR].astype(BF16)
            u_ref[OUTER + start + k] = spec[INNER:, PAIR * k : PAIR * k + PAIR].astype(BF16)
            back_ref[start + k] = back[:INNER, PAIR * k : PAIR * k + PAIR]
            back_ref[OUTER + start + k] = back[INNER:, PAIR * k : PAIR * k + PAIR]

    slabs(body, 4)

    @pl.loop(0, 8)
    def _(p):
        row = pl.multiple_of(p * 16, 16)
        gain = gain_ref[...]
        given = v_ref[:, :, pl.ds(row, 16), :].astype(F32)
        out = [[], []]
        for h in range(2):
            held = back_ref[:, pl.ds(row + 8 * h, 8), :].reshape(512, PAIR).astype(BF16)
            lines = dot(last_ref[2 * p + h], held).reshape(OUTER, 8, PAIR)
            for a in range(2):
                out[a].append(
                    lines[:, :, LANES * a : LANES * a + LANES]
                    + gain * given[:, a, 8 * h : 8 * h + 8]
                )
        for a in range(2):
            out_ref[:, a, pl.ds(row, 16), :] = jnp.concatenate(out[a], 1).astype(BF16)


def filter_grad_kernel(
    spec_ref, two_ref, member_ref, three_ref, three_zero_ref, turn_cos_ref, turn_sin_ref, grad_ref,
    filter_ref, sum_ref,
):
    sum_ref[...] = jnp.zeros_like(sum_ref)

    def body(start, count, packed):
        for k in range(count):
            real = spec_ref[start + k].astype(F32)
            imag = spec_ref[OUTER + start + k].astype(F32)
            fr, fi = times(
                real[:, :LANES], imag[:, :LANES], real[:, LANES:], imag[:, LANES:], True, packed
            )
            both = jnp.concatenate([fr, fi], 0)
            high = both.astype(BF16)
            rest = (both - high.astype(F32)).astype(BF16)
            slab = start + k
            member = member_ref[(slab // 2) % 8, pl.ds(LANES * (slab % 2), LANES), :]
            sum_ref[slab // 16] += dot(high, member) + dot(rest, member)

    slabs(body, 4)
    total = jnp.concatenate([sum_ref[0], sum_ref[1]], 1).astype(BF16)
    back = dot(three_ref[...], total)
    back_zero = dot(three_zero_ref[...], total)
    packed = lax.broadcasted_iota(jnp.int32, back.shape, 1) < 8
    back = jnp.where(packed, back_zero, back)
    br, bi = back[:INNER], back[INNER:]
    c, s = turn_cos_ref[...], turn_sin_ref[...]
    turned = jnp.concatenate([br * c - bi * s, br * s + bi * c], 1).astype(BF16)
    filter_ref[...] = dot(turned, grad_ref[...]).T


def gather_kernel(gate_ref, input_ref, cotan_ref, out_ref):
    for k in range(out_ref.shape[0]):
        cut = slice(LANES * k, LANES * k + LANES)
        out_ref[k, 0] = input_ref[:, cut]
        product = cotan_ref[:, cut].astype(F32) * gate_ref[:, cut].astype(F32)
        out_ref[k, 1] = product.astype(BF16)


def spread_kernel(back_ref, cotan_ref, gate_grad_ref, input_grad_ref):
    for k in range(back_ref.shape[0]):
        cut = slice(LANES * k, LANES * k + LANES)
        product = cotan_ref[:, cut].astype(F32) * back_ref[k, 0].astype(F32)
        gate_grad_ref[:, cut] = product.astype(BF16)
        input_grad_ref[:, cut] = back_ref[k, 1]


STEPS = 8
ROWS_BLOCK = pl.BlockSpec((INNER, OUTER // STEPS * LANES), lambda i: (0, i))
MOVED_BLOCK = pl.BlockSpec((OUTER // STEPS, 2, INNER, LANES), lambda i: (i, 0, 0, 0))
MOVED = jax.ShapeDtypeStruct((OUTER, 2, INNER, LANES), BF16)
ROWS = jax.ShapeDtypeStruct((INNER, OUTER * LANES), BF16)
HELD = jax.ShapeDtypeStruct((2 * OUTER, INNER, PAIR), BF16)


def gather(gate, given, cotan):
    return pl.pallas_call(
        gather_kernel,
        grid=(STEPS,),
        out_shape=MOVED,
        in_specs=[ROWS_BLOCK] * 3,
        out_specs=MOVED_BLOCK,
        compiler_params=pltpu.CompilerParams(vmem_limit_bytes=8 << 20),
    )(gate, given, cotan)


def spread(back, cotan):
    return pl.pallas_call(
        spread_kernel,
        grid=(STEPS,),
        out_shape=(ROWS, ROWS),
        in_specs=[MOVED_BLOCK, ROWS_BLOCK],
        out_specs=(ROWS_BLOCK, ROWS_BLOCK),
        compiler_params=pltpu.CompilerParams(vmem_limit_bytes=8 << 20),
    )(back, cotan)


def call(kernel, operands, outs, scratch, flops, limit):
    space = pl.BlockSpec(memory_space=pltpu.VMEM)
    return pl.pallas_call(
        kernel,
        out_shape=outs,
        in_specs=[space] * len(operands),
        out_specs=jax.tree.map(lambda _: space, outs),
        scratch_shapes=scratch,
        compiler_params=pltpu.CompilerParams(vmem_limit_bytes=limit),
        cost_estimate=pl.CostEstimate(flops=flops, bytes_accessed=16 << 20, transcendentals=0),
    )(*operands)


def filter_spectrum(t, laid):
    return call(
        filter_kernel,
        (laid, t["one"], t["two"], t["two_zero"]),
        jax.ShapeDtypeStruct((2 * OUTER, INNER, LANES), F32),
        [pltpu.VMEM((2 * OUTER, INNER, LANES), BF16)],
        4 << 30, 24 << 20,
    )


def main_path(t, moved, kernel_spec, gains):
    return call(
        main_kernel,
        (moved, kernel_spec, gains, t["one"], t["two"], t["two_zero"], t["three"],
         t["three_zero"], t["last"]),
        (MOVED, HELD),
        [pltpu.VMEM((2 * OUTER, INNER, PAIR), F32)],
        6 << 30, 40 << 20,
    )


def filter_gradient(t, spec):
    return call(
        filter_grad_kernel,
        (spec, t["two"], t["member"], t["three"], t["three_zero"], t["turn_cos"], t["turn_sin"],
         t["grad"]),
        jax.ShapeDtypeStruct((PAIR, LANES), F32),
        [pltpu.VMEM((2, PAIR, LANES), F32)],
        2 << 30, 16 << 20,
    )


def lay_filters(filters):
    groups = filters.shape[0]
    member = np.repeat(np.eye(groups), LANES // groups, axis=1)
    return jnp.einsum(
        "gt,gc->tc", filters, jnp.asarray(member, BF16), preferred_element_type=F32
    ).astype(BF16).reshape(OUTER, INNER, LANES)


def exchange(blocks):
    return lax.all_to_all(blocks, "ctx", split_axis=0, concat_axis=0, tiled=True)


def sum_over_sequences(parts):
    count = lax.axis_size("dp")
    place = lax.axis_index("dp")

    def share(owner):
        return lax.dynamic_index_in_dim(parts, owner, 0, keepdims=False)

    total = share(place)
    for hop in range(1, count):
        total = total + lax.ppermute(
            share((place + hop) % count), "dp", [(i, (i + hop) % count) for i in range(count)]
        )
    return total


def unit(moved_input, moved_grad, filters, gains):
    t = build_tables(1.0 / (8192 * 512))
    moved = jnp.stack([moved_input, moved_grad], 1)
    out, spec = main_path(t, moved, filter_spectrum(t, lay_filters(filters)), gains)
    return out[:, 0], out[:, 1], filter_gradient(t, spec)


def on_device(gate_values, conv_input, cotangent, filters, direct_scale):
    replica_count = lax.axis_size("dp")
    grad_scale = 1.0 / (POINTS * math.sqrt(GROUP_WIDTH * replica_count * POINTS // 2))
    t = build_tables(grad_scale)
    moved = exchange(gather(gate_values[0], conv_input[0], cotangent[0]))
    kernel_spec = filter_spectrum(t, lay_filters(filters))
    out, spec = main_path(t, moved, kernel_spec, direct_scale[None, :])
    back = exchange(out)
    filter_part = filter_gradient(t, spec)
    filter_grad = sum_over_sequences(filter_part.reshape(replica_count, -1, LANES))
    filter_grad = filter_grad.reshape(filters.shape[0], -1)
    gate_grad, input_grad = spread(back, cotangent[0])
    return gate_grad[None], input_grad[None], filter_grad


def solution(mesh):
    placed = (
        P("dp", "ctx", None),
        P("dp", "ctx", None),
        P("dp", "ctx", None),
        P("ctx", None),
        P("ctx"),
    )
    return jax.shard_map(
        on_device,
        mesh=mesh,
        in_specs=placed,
        out_specs=(P("dp", "ctx", None), P("dp", "ctx", None), P("ctx", "dp")),
        check_vma=False,
    )
```

```python
import math

import jax
import jax.numpy as jnp
import numpy as np
from jax import lax
from jax.experimental import pallas as pl
from jax.experimental.pallas import tpu as pltpu
from jax.sharding import PartitionSpec as P

GROUP_WIDTH = 16
OUTER = 32
INNER = 128
POINTS = 8192
LANES = 128
PAIR = 2 * LANES
F32 = jnp.float32
BF16 = jnp.bfloat16


def turns(numerator, denominator):
    angle = 2.0 * np.pi * (np.asarray(numerator) % denominator) / denominator
    return np.cos(angle), np.sin(angle)


def build_tables(grad_scale):
    eye = np.eye(8)
    slab = np.arange(OUTER)[:, None, None]
    outer = np.arange(OUTER)[None, :, None]
    step = np.arange(INNER)[None, None, :]
    cos_part, sin_part = turns(slab * (128 * outer + step), POINTS)
    first = np.concatenate([cos_part, -sin_part], 0)
    first[0] = 1.0
    first[OUTER] = (1.0 - 2.0 * (np.arange(OUTER) % 2))[:, None]
    table_one = np.einsum("rnqs,st->qrtns", first.reshape(64, OUTER, 16, 8), eye)
    table_one = table_one.reshape(16, 512, 256)
    table_last = table_one.transpose(0, 2, 1) * (2.0 / POINTS)

    index = np.arange(INNER)
    cos_two, sin_two = turns(index[:, None] * index[None, :], INNER)
    table_two = np.block([[cos_two, sin_two], [-sin_two, cos_two]])
    half = np.arange(64)
    cos_low, sin_low = turns(half[:, None] * index[None, :], INNER)
    cos_mid, sin_mid = turns((32 + 64 * half[:, None]) * index[None, :], POINTS)
    zero = np.zeros((64, INNER))
    sin_low = -sin_low
    sin_low[0] = 1.0 - 2.0 * (index % 2)
    table_two_zero = np.block(
        [[cos_low, zero], [zero, cos_mid], [sin_low, zero], [zero, -sin_mid]]
    )
    weight = np.ones((256, 1))
    weight[0] = 0.5
    weight[128] = 0.5
    mixed_rows = np.arange(256).reshape(2, 16, 8).transpose(1, 0, 2).reshape(256)
    table_three = table_two.T[:, mixed_rows]
    table_three_zero = (table_two_zero * weight).T[:, mixed_rows]
    table_two = table_two[mixed_rows]
    table_two_zero = table_two_zero[mixed_rows]

    member = np.zeros((8, 256, LANES))
    for pair in range(8):
        for side in range(2):
            for channel in range(LANES):
                lane = (2 * pair + side) * 8 + channel // GROUP_WIDTH
                member[pair, side * LANES + channel, lane] = 1.0
    slab_lane = np.repeat(np.arange(OUTER), 8)
    group_lane = np.tile(np.arange(8), OUTER)
    turn_cos, turn_sin = turns(index[:, None] * slab_lane[None, :], POINTS)
    last_cos, last_sin = turns(slab_lane[:, None] * np.arange(OUTER)[None, :], 64)
    last_sin = -last_sin
    last_sin[slab_lane == 0] = 1.0 - 2.0 * (np.arange(OUTER) % 2)
    parts = np.stack([last_cos, last_sin])
    same = group_lane[:, None] == np.arange(8)[None, :]
    table_grad = np.einsum("pln,lg->plgn", parts, same)
    table_grad = table_grad.reshape(2, 256, 8, 4, 8).transpose(0, 1, 3, 2, 4)
    table_grad = table_grad.reshape(512, 256) * (2.0 * grad_scale)

    def low(values):
        return jnp.asarray(values, BF16)

    def wide(values):
        return jnp.asarray(values, F32)

    return dict(
        one=low(table_one),
        last=low(table_last),
        inner=low(np.stack([table_two, table_two_zero, table_three, table_three_zero])),
        member=low(member),
        turn_cos=wide(turn_cos),
        turn_sin=wide(turn_sin),
        grad=low(table_grad),
    )


def dot(left, right):
    return jnp.dot(left, right, preferred_element_type=F32)


def outer_block(given, one_ref, p, u_ref):
    lanes = given.shape[2]
    out = []
    for h in range(2):
        held = given[:, 8 * h : 8 * h + 8].reshape(256, lanes).astype(BF16)
        out.append(dot(one_ref[2 * p + h], held).reshape(64, 8, lanes))
    both = jnp.concatenate(out, 1).astype(BF16)
    row = pl.multiple_of(p * 16, 16)
    u_ref[:, pl.ds(row, 16), :] = both[:OUTER]
    u_ref[:, pl.ds(INNER + row, 16), :] = both[OUTER:]


def apart(values):
    values = values.reshape(16, 2, 8, values.shape[1])
    return values[:, 0], values[:, 1]


def together(real, imag):
    return jnp.stack([real, imag], 1).reshape(256, real.shape[2])


def times(ar, ai, br, bi, conjugate, packed):
    cross = ai * bi
    if conjugate:
        real, imag = ar * br + cross, ar * bi - ai * br
    else:
        real, imag = ar * br - cross, ar * bi + ai * br
    if packed:
        place = lax.broadcasted_iota(jnp.int32, ar.shape, 0) * 8
        edge = place + lax.broadcasted_iota(jnp.int32, ar.shape, 1) == 0
        real = jnp.where(edge, ar * br, real)
        imag = jnp.where(edge, cross, imag)
    return real, imag


def lane_cut(values, k, width):
    return values[:, width * k : width * k + width]


def slabs(body, count):
    body(0, 1, True)
    body(1, count - 1, False)

    @pl.loop(1, OUTER // count)
    def _(m):
        body(count * m, count, False)


def filter_kernel(v_ref, one_ref, inner_ref, spec_ref, u_ref):
    @pl.loop(0, 8)
    def _(p):
        row = pl.multiple_of(p * 16, 16)
        outer_block(v_ref[:, pl.ds(row, 16), :].astype(F32), one_ref, p, u_ref)

    def body(start, count, packed):
        held = jnp.concatenate([u_ref[start + k] for k in range(count)], 1)
        spec = dot(inner_ref[int(packed)], held)
        for k in range(count):
            spec_ref[start + k] = lane_cut(spec, k, LANES)

    slabs(body, 4)


def main_kernel(
    v_hbm, h_hbm, gain_hbm, one_hbm, inner_hbm, last_hbm, out_hbm, spec_hbm,
    v_ref, h_ref, gain_ref, one_ref, inner_ref, last_ref, out_ref, u_ref, back_ref,
    v_sem, h_sem, gain_sem, one_sem, inner_sem, last_sem, out_sem, spec_sem,
):
    def v_copy(p):
        cut = pl.ds(pl.multiple_of(p * 16, 16), 16)
        return pltpu.make_async_copy(v_hbm.at[:, :, cut], v_ref.at[:, :, cut], v_sem.at[p])

    def out_copy(p):
        cut = pl.ds(pl.multiple_of(p * 16, 16), 16)
        return pltpu.make_async_copy(out_ref.at[:, :, cut], out_hbm.at[:, :, cut], out_sem.at[p])

    def table_copy(hbm, ref, sem, p):
        cut = pl.ds(2 * p, 2)
        return pltpu.make_async_copy(hbm.at[cut], ref.at[cut], sem.at[p])

    def slab_copy(source, target, sem, m):
        cut = pl.ds(4 * m, 4)
        return pltpu.make_async_copy(source.at[cut], target.at[cut], sem.at[m])

    inner_copy = pltpu.make_async_copy(inner_hbm, inner_ref, inner_sem)
    gain_copy = pltpu.make_async_copy(gain_hbm, gain_ref, gain_sem)

    @pl.loop(0, 8)
    def _(p):
        v_copy(p).start()
        table_copy(one_hbm, one_ref, one_sem, p).start()

    inner_copy.start()
    gain_copy.start()

    @pl.loop(0, 8)
    def _(p):
        slab_copy(h_hbm, h_ref, h_sem, p).start()
        table_copy(last_hbm, last_ref, last_sem, p).start()
        v_copy(p).wait()
        table_copy(one_hbm, one_ref, one_sem, p).wait()
        row = pl.multiple_of(p * 16, 16)
        both = v_ref[:, :, pl.ds(row, 16), :].astype(F32)
        outer_block(jnp.concatenate([both[:, 0], both[:, 1]], 2), one_ref, p, u_ref)

    inner_copy.wait()

    def body(start, count, packed):
        held = jnp.concatenate([u_ref[start + k] for k in range(count)], 1)
        spec = dot(inner_ref[int(packed)], held)
        real, imag = apart(spec)
        out_real, out_imag = [], []
        for k in range(count):
            hr, hi = apart(h_ref[start + k])
            low = slice(PAIR * k, PAIR * k + LANES)
            high = slice(PAIR * k + LANES, PAIR * k + PAIR)
            pr, pi = times(hr, hi, real[..., low], imag[..., low], False, packed)
            ar, ai = times(hr, hi, real[..., high], imag[..., high], True, packed)
            out_real += [pr, ar]
            out_imag += [pi, ai]
        product = together(jnp.concatenate(out_real, 2), jnp.concatenate(out_imag, 2))
        back = dot(inner_ref[2 + int(packed)], product.astype(BF16))
        for k in range(count):
            u_ref[start + k] = lane_cut(spec, k, PAIR).astype(BF16)
            back_ref[start + k] = lane_cut(back, k, PAIR)

    slab_copy(h_hbm, h_ref, h_sem, 0).wait()
    body(0, 1, True)
    body(1, 3, False)
    slab_copy(u_ref, spec_hbm, spec_sem, 0).start()

    @pl.loop(1, 8)
    def _(m):
        slab_copy(h_hbm, h_ref, h_sem, m).wait()
        body(4 * m, 4, False)
        slab_copy(u_ref, spec_hbm, spec_sem, m).start()

    gain_copy.wait()

    @pl.loop(0, 8)
    def _(p):
        table_copy(last_hbm, last_ref, last_sem, p).wait()
        row = pl.multiple_of(p * 16, 16)
        gain = gain_ref[...]
        given = v_ref[:, :, pl.ds(row, 16), :].astype(F32)
        out = [[], []]
        for h in range(2):
            held = jnp.concatenate(
                [
                    back_ref[:, pl.ds(INNER * part + row + 8 * h, 8), :].reshape(256, PAIR)
                    for part in range(2)
                ],
                0,
            ).astype(BF16)
            lines = dot(last_ref[2 * p + h], held).reshape(OUTER, 8, PAIR)
            for a in range(2):
                out[a].append(
                    lines[:, :, LANES * a : LANES * a + LANES]
                    + gain * given[:, a, 8 * h : 8 * h + 8]
                )
        for a in range(2):
            out_ref[:, a, pl.ds(row, 16), :] = jnp.concatenate(out[a], 1).astype(BF16)
        out_copy(p).start()

    @pl.loop(0, 8)
    def _(p):
        slab_copy(u_ref, spec_hbm, spec_sem, p).wait()
        out_copy(p).wait()


def filter_grad_kernel(
    spec_ref, inner_ref, member_ref, turn_cos_ref, turn_sin_ref, grad_ref, filter_ref, sum_ref
):
    sum_ref[...] = jnp.zeros_like(sum_ref)

    def body(start, count, packed):
        for k in range(count):
            real, imag = apart(spec_ref[start + k].astype(F32))
            both = together(
                *times(
                    real[..., :LANES], imag[..., :LANES], real[..., LANES:], imag[..., LANES:],
                    True, packed,
                )
            )
            high = both.astype(BF16)
            rest = (both - high.astype(F32)).astype(BF16)
            slab = start + k
            member = member_ref[(slab // 2) % 8, pl.ds(LANES * (slab % 2), LANES), :]
            sum_ref[slab // 16] += dot(high, member) + dot(rest, member)

    slabs(body, 4)
    total = jnp.concatenate([sum_ref[0], sum_ref[1]], 1).astype(BF16)
    back = dot(inner_ref[2], total)
    back_zero = dot(inner_ref[3], total)
    packed = lax.broadcasted_iota(jnp.int32, back.shape, 1) < 8
    back = jnp.where(packed, back_zero, back)
    br, bi = back[:INNER], back[INNER:]
    c, s = turn_cos_ref[...], turn_sin_ref[...]
    turned = jnp.concatenate([br * c - bi * s, br * s + bi * c], 1).astype(BF16)
    filter_ref[...] = dot(turned, grad_ref[...]).T


def gather_kernel(gate_ref, input_ref, cotan_ref, out_ref):
    for k in range(out_ref.shape[0]):
        cut = slice(LANES * k, LANES * k + LANES)
        out_ref[k, 0] = input_ref[:, cut]
        product = cotan_ref[:, cut].astype(F32) * gate_ref[:, cut].astype(F32)
        out_ref[k, 1] = product.astype(BF16)


def spread_kernel(back_ref, cotan_ref, gate_grad_ref, input_grad_ref):
    for k in range(back_ref.shape[0]):
        cut = slice(LANES * k, LANES * k + LANES)
        product = cotan_ref[:, cut].astype(F32) * back_ref[k, 0].astype(F32)
        gate_grad_ref[:, cut] = product.astype(BF16)
        input_grad_ref[:, cut] = back_ref[k, 1]


STEPS = 4
ROWS_BLOCK = pl.BlockSpec((INNER, OUTER // STEPS * LANES), lambda i: (0, i))
MOVED_BLOCK = pl.BlockSpec((OUTER // STEPS, 2, INNER, LANES), lambda i: (i, 0, 0, 0))
MOVED = jax.ShapeDtypeStruct((OUTER, 2, INNER, LANES), BF16)
ROWS = jax.ShapeDtypeStruct((INNER, OUTER * LANES), BF16)
HELD = jax.ShapeDtypeStruct((OUTER, PAIR, PAIR), BF16)


def gather(gate, given, cotan):
    return pl.pallas_call(
        gather_kernel,
        grid=(STEPS,),
        out_shape=MOVED,
        in_specs=[ROWS_BLOCK] * 3,
        out_specs=MOVED_BLOCK,
        compiler_params=pltpu.CompilerParams(vmem_limit_bytes=60 << 20),
    )(gate, given, cotan)


def spread(back, cotan):
    return pl.pallas_call(
        spread_kernel,
        grid=(STEPS,),
        out_shape=(ROWS, ROWS),
        in_specs=[MOVED_BLOCK, ROWS_BLOCK],
        out_specs=(ROWS_BLOCK, ROWS_BLOCK),
        compiler_params=pltpu.CompilerParams(vmem_limit_bytes=60 << 20),
    )(back, cotan)


def call(kernel, operands, outs, scratch, flops, limit):
    space = pl.BlockSpec(memory_space=pltpu.VMEM)
    return pl.pallas_call(
        kernel,
        out_shape=outs,
        in_specs=[space] * len(operands),
        out_specs=jax.tree.map(lambda _: space, outs),
        scratch_shapes=scratch,
        compiler_params=pltpu.CompilerParams(vmem_limit_bytes=limit),
        cost_estimate=pl.CostEstimate(flops=flops, bytes_accessed=16 << 20, transcendentals=0),
    )(*operands)


def filter_spectrum(t, laid):
    return call(
        filter_kernel,
        (laid, t["one"], t["inner"]),
        jax.ShapeDtypeStruct((OUTER, PAIR, LANES), F32),
        [pltpu.VMEM((OUTER, PAIR, LANES), BF16)],
        4 << 30, 24 << 20,
    )


def main_path(t, moved, kernel_spec, gains):
    operands = (moved, kernel_spec, gains, t["one"], t["inner"], t["last"])
    space = pl.BlockSpec(memory_space=pltpu.HBM)
    sems = pltpu.SemaphoreType.DMA
    return pl.pallas_call(
        main_kernel,
        out_shape=(MOVED, HELD),
        in_specs=[space] * len(operands),
        out_specs=(space, space),
        scratch_shapes=[pltpu.VMEM(o.shape, o.dtype) for o in operands]
        + [
            pltpu.VMEM(MOVED.shape, BF16),
            pltpu.VMEM(HELD.shape, BF16),
            pltpu.VMEM(HELD.shape, F32),
            sems((8,)), sems((8,)), sems, sems((8,)), sems, sems((8,)), sems((8,)), sems((8,)),
        ],
        compiler_params=pltpu.CompilerParams(vmem_limit_bytes=48 << 20),
        cost_estimate=pl.CostEstimate(
            flops=6 << 30, bytes_accessed=20 << 20, transcendentals=0
        ),
    )(*operands)


def filter_gradient(t, spec):
    return call(
        filter_grad_kernel,
        (spec, t["inner"], t["member"], t["turn_cos"], t["turn_sin"], t["grad"]),
        jax.ShapeDtypeStruct((PAIR, LANES), F32),
        [pltpu.VMEM((2, PAIR, LANES), F32)],
        2 << 30, 16 << 20,
    )


def lay_filters(filters):
    groups = filters.shape[0]
    member = np.repeat(np.eye(groups), LANES // groups, axis=1)
    return jnp.einsum(
        "gt,gc->tc", filters, jnp.asarray(member, BF16), preferred_element_type=F32
    ).astype(BF16).reshape(OUTER, INNER, LANES)


def exchange(blocks):
    return lax.all_to_all(blocks, "ctx", split_axis=0, concat_axis=0, tiled=True)


def sum_over_sequences(parts):
    count = lax.axis_size("dp")
    place = lax.axis_index("dp")

    def share(owner):
        return lax.dynamic_index_in_dim(parts, owner, 0, keepdims=False)

    total = share(place)
    for hop in range(1, count):
        total = total + lax.ppermute(
            share((place + hop) % count), "dp", [(i, (i + hop) % count) for i in range(count)]
        )
    return total


def unit(moved_input, moved_grad, filters, gains):
    t = build_tables(1.0 / (8192 * 512))
    moved = jnp.stack([moved_input, moved_grad], 1)
    out, spec = main_path(t, moved, filter_spectrum(t, lay_filters(filters)), gains)
    return out[:, 0], out[:, 1], filter_gradient(t, spec)


def on_device(gate_values, conv_input, cotangent, filters, direct_scale):
    replica_count = lax.axis_size("dp")
    grad_scale = 1.0 / (POINTS * math.sqrt(GROUP_WIDTH * replica_count * POINTS // 2))
    t = build_tables(grad_scale)
    moved = exchange(gather(gate_values[0], conv_input[0], cotangent[0]))
    kernel_spec = filter_spectrum(t, lay_filters(filters))
    out, spec = main_path(t, moved, kernel_spec, direct_scale[None, :])
    back = exchange(out)
    filter_part = filter_gradient(t, spec)
    filter_grad = sum_over_sequences(filter_part.reshape(replica_count, -1, LANES))
    filter_grad = filter_grad.reshape(filters.shape[0], -1)
    gate_grad, input_grad = spread(back, cotangent[0])
    return gate_grad[None], input_grad[None], filter_grad


def solution(mesh):
    placed = (
        P("dp", "ctx", None),
        P("dp", "ctx", None),
        P("dp", "ctx", None),
        P("ctx", None),
        P("ctx"),
    )
    return jax.shard_map(
        on_device,
        mesh=mesh,
        in_specs=placed,
        out_specs=(P("dp", "ctx", None), P("dp", "ctx", None), P("ctx", "dp")),
        check_vma=False,
    )
```

```python
import math

import jax
import jax.numpy as jnp
import numpy as np
from jax import lax
from jax.experimental import pallas as pl
from jax.experimental.pallas import tpu as pltpu
from jax.sharding import PartitionSpec as P

GROUP_WIDTH = 16
OUTER = 32
INNER = 128
POINTS = 8192
LANES = 128
PAIR = 2 * LANES
F32 = jnp.float32
BF16 = jnp.bfloat16


def turns(numerator, denominator):
    angle = 2.0 * np.pi * (np.asarray(numerator) % denominator) / denominator
    return np.cos(angle), np.sin(angle)


def build_tables(grad_scale):
    eye = np.eye(8)
    slab = np.arange(OUTER)[:, None, None]
    outer = np.arange(OUTER)[None, :, None]
    step = np.arange(INNER)[None, None, :]
    cos_part, sin_part = turns(slab * (128 * outer + step), POINTS)
    first = np.concatenate([cos_part, -sin_part], 0)
    first[0] = 1.0
    first[OUTER] = (1.0 - 2.0 * (np.arange(OUTER) % 2))[:, None]
    table_one = np.einsum("rnqs,st->qrtns", first.reshape(64, OUTER, 16, 8), eye)
    table_one = table_one.reshape(16, 512, 256)
    table_last = table_one.transpose(0, 2, 1) * (2.0 / POINTS)

    index = np.arange(INNER)
    cos_two, sin_two = turns(index[:, None] * index[None, :], INNER)
    table_two = np.block([[cos_two, sin_two], [-sin_two, cos_two]])
    half = np.arange(64)
    cos_low, sin_low = turns(half[:, None] * index[None, :], INNER)
    cos_mid, sin_mid = turns((32 + 64 * half[:, None]) * index[None, :], POINTS)
    zero = np.zeros((64, INNER))
    sin_low = -sin_low
    sin_low[0] = 1.0 - 2.0 * (index % 2)
    table_two_zero = np.block(
        [[cos_low, zero], [zero, cos_mid], [sin_low, zero], [zero, -sin_mid]]
    )
    weight = np.ones((256, 1))
    weight[0] = 0.5
    weight[128] = 0.5
    mixed_rows = np.arange(256).reshape(2, 16, 8).transpose(1, 0, 2).reshape(256)
    table_three = table_two.T[:, mixed_rows]
    table_three_zero = (table_two_zero * weight).T[:, mixed_rows]
    table_two = table_two[mixed_rows]
    table_two_zero = table_two_zero[mixed_rows]

    member = np.zeros((8, 256, LANES))
    for pair in range(8):
        for side in range(2):
            for channel in range(LANES):
                lane = (2 * pair + side) * 8 + channel // GROUP_WIDTH
                member[pair, side * LANES + channel, lane] = 1.0
    slab_lane = np.repeat(np.arange(OUTER), 8)
    group_lane = np.tile(np.arange(8), OUTER)
    turn_cos, turn_sin = turns(index[:, None] * slab_lane[None, :], POINTS)
    last_cos, last_sin = turns(slab_lane[:, None] * np.arange(OUTER)[None, :], 64)
    last_sin = -last_sin
    last_sin[slab_lane == 0] = 1.0 - 2.0 * (np.arange(OUTER) % 2)
    parts = np.stack([last_cos, last_sin])
    same = group_lane[:, None] == np.arange(8)[None, :]
    table_grad = np.einsum("pln,lg->plgn", parts, same)
    table_grad = table_grad.reshape(2, 256, 8, 4, 8).transpose(0, 1, 3, 2, 4)
    table_grad = table_grad.reshape(512, 256) * (2.0 * grad_scale)

    def low(values):
        return jnp.asarray(values, BF16)

    def wide(values):
        return jnp.asarray(values, F32)

    return dict(
        one=low(table_one),
        last=low(table_last),
        inner=low(np.stack([table_two, table_two_zero, table_three, table_three_zero])),
        member=low(member),
        turn_cos=wide(turn_cos),
        turn_sin=wide(turn_sin),
        grad=low(table_grad),
    )


def dot(left, right):
    return jnp.dot(left, right, preferred_element_type=F32)


def outer_block(given, one_ref, p, u_ref):
    lanes = given.shape[2]
    out = []
    for h in range(2):
        held = given[:, 8 * h : 8 * h + 8].reshape(256, lanes).astype(BF16)
        out.append(dot(one_ref[2 * p + h], held).reshape(64, 8, lanes))
    both = jnp.concatenate(out, 1).astype(BF16)
    row = p * 16 if isinstance(p, int) else pl.multiple_of(p * 16, 16)
    u_ref[:, pl.ds(row, 16), :] = both[:OUTER]
    u_ref[:, pl.ds(INNER + row, 16), :] = both[OUTER:]


def apart(values):
    values = values.reshape(16, 2, 8, values.shape[1])
    return values[:, 0], values[:, 1]


def together(real, imag):
    return jnp.stack([real, imag], 1).reshape(256, real.shape[2])


def times(ar, ai, br, bi, conjugate, packed):
    cross = ai * bi
    if conjugate:
        real, imag = ar * br + cross, ar * bi - ai * br
    else:
        real, imag = ar * br - cross, ar * bi + ai * br
    if packed:
        place = lax.broadcasted_iota(jnp.int32, ar.shape, 0) * 8
        edge = place + lax.broadcasted_iota(jnp.int32, ar.shape, 1) == 0
        real = jnp.where(edge, ar * br, real)
        imag = jnp.where(edge, cross, imag)
    return real, imag


def lane_cut(values, k, width):
    return values[:, width * k : width * k + width]


def slabs(body, count):
    body(0, 1, True)
    body(1, count - 1, False)

    @pl.loop(1, OUTER // count)
    def _(m):
        body(count * m, count, False)


OUTER_AT_ONCE = 2
SLABS_AT_ONCE = 2
LAST_AT_ONCE = 2


def several(count, body, first=0):
    if count - first <= 1:
        for g in range(first, count):
            body(g)
    else:
        pl.loop(first, count)(body)


def filter_kernel(v_ref, one_ref, inner_ref, spec_ref, u_ref):
    @pl.loop(0, 8)
    def _(p):
        row = pl.multiple_of(p * 16, 16)
        outer_block(v_ref[:, pl.ds(row, 16), :].astype(F32), one_ref, p, u_ref)

    def body(start, count, packed):
        held = jnp.concatenate([u_ref[start + k] for k in range(count)], 1)
        spec = dot(inner_ref[int(packed)], held)
        for k in range(count):
            spec_ref[start + k] = lane_cut(spec, k, LANES)

    slabs(body, 4)


def main_kernel(
    v_ref, h_hbm, gain_hbm, one_hbm, inner_hbm, last_hbm, out_hbm, spec_hbm,
    h_ref, gain_ref, one_ref, inner_ref, last_ref, out_ref, u_ref, back_ref,
    h_sem, gain_sem, one_sem, inner_sem, last_sem, out_sem, spec_sem,
):
    def table_copy(hbm, ref, sem, p):
        cut = pl.ds(2 * p, 2)
        return pltpu.make_async_copy(hbm.at[cut], ref.at[cut], sem.at[p])

    def slab_copy(source, target, sem, m):
        cut = pl.ds(4 * m, 4)
        return pltpu.make_async_copy(source.at[cut], target.at[cut], sem.at[m])

    inner_copy = pltpu.make_async_copy(inner_hbm, inner_ref, inner_sem)
    gain_copy = pltpu.make_async_copy(gain_hbm, gain_ref, gain_sem)

    @pl.loop(0, 8)
    def _(p):
        table_copy(one_hbm, one_ref, one_sem, p).start()

    inner_copy.start()
    gain_copy.start()

    @pl.loop(0, 8)
    def _(p):
        slab_copy(h_hbm, h_ref, h_sem, p).start()

    @pl.loop(0, 8)
    def _(p):
        table_copy(last_hbm, last_ref, last_sem, p).start()

    def outer_group(g):
        for k in range(OUTER_AT_ONCE):
            table_copy(one_hbm, one_ref, one_sem, g * OUTER_AT_ONCE + k).wait()
        for k in range(OUTER_AT_ONCE):
            p = g * OUTER_AT_ONCE + k
            row = p * 16 if isinstance(p, int) else pl.multiple_of(p * 16, 16)
            both = v_ref[:, :, pl.ds(row, 16), :].astype(F32)
            outer_block(jnp.concatenate([both[:, 0], both[:, 1]], 2), one_ref, p, u_ref)

    several(8 // OUTER_AT_ONCE, outer_group)
    inner_copy.wait()

    def body(start, count, packed):
        held = jnp.concatenate([u_ref[start + k] for k in range(count)], 1)
        spec = dot(inner_ref[int(packed)], held)
        real, imag = apart(spec)
        out_real, out_imag = [], []
        for k in range(count):
            hr, hi = apart(h_ref[start + k])
            low = slice(PAIR * k, PAIR * k + LANES)
            high = slice(PAIR * k + LANES, PAIR * k + PAIR)
            pr, pi = times(hr, hi, real[..., low], imag[..., low], False, packed)
            ar, ai = times(hr, hi, real[..., high], imag[..., high], True, packed)
            out_real += [pr, ar]
            out_imag += [pi, ai]
        product = together(jnp.concatenate(out_real, 2), jnp.concatenate(out_imag, 2))
        back = dot(inner_ref[2 + int(packed)], product.astype(BF16))
        for k in range(count):
            u_ref[start + k] = lane_cut(spec, k, PAIR).astype(BF16)
            back_ref[start + k] = lane_cut(back, k, PAIR)

    def slab_group(g):
        for k in range(SLABS_AT_ONCE):
            slab_copy(h_hbm, h_ref, h_sem, g * SLABS_AT_ONCE + k).wait()
        for k in range(SLABS_AT_ONCE):
            m = g * SLABS_AT_ONCE + k
            if isinstance(m, int) and m == 0:
                body(0, 1, True)
                body(1, 3, False)
            else:
                body(4 * m, 4, False)
        for k in range(SLABS_AT_ONCE):
            slab_copy(u_ref, spec_hbm, spec_sem, g * SLABS_AT_ONCE + k).start()

    slab_group(0)
    several(8 // SLABS_AT_ONCE, slab_group, 1)
    gain_copy.wait()

    def last_group(g):
        for k in range(LAST_AT_ONCE):
            table_copy(last_hbm, last_ref, last_sem, g * LAST_AT_ONCE + k).wait()
        for k in range(LAST_AT_ONCE):
            last_block(g * LAST_AT_ONCE + k)
        for k in range(LAST_AT_ONCE):
            block_copy(out_ref, out_hbm, out_sem, g * LAST_AT_ONCE + k, 16).start()

    def last_block(p):
        row = p * 16 if isinstance(p, int) else pl.multiple_of(p * 16, 16)
        gain = gain_ref[...]
        given = v_ref[:, :, pl.ds(row, 16), :].astype(F32)
        out = [[], []]
        for h in range(2):
            held = jnp.concatenate(
                [
                    back_ref[:, pl.ds(INNER * part + row + 8 * h, 8), :].reshape(256, PAIR)
                    for part in range(2)
                ],
                0,
            ).astype(BF16)
            lines = dot(last_ref[2 * p + h], held).reshape(OUTER, 8, PAIR)
            for a in range(2):
                out[a].append(
                    lines[:, :, LANES * a : LANES * a + LANES]
                    + gain * given[:, a, 8 * h : 8 * h + 8]
                )
        for a in range(2):
            out_ref[:, a, pl.ds(row, 16), :] = jnp.concatenate(out[a], 1).astype(BF16)

    several(8 // LAST_AT_ONCE, last_group)

    @pl.loop(0, 8)
    def _(p):
        slab_copy(u_ref, spec_hbm, spec_sem, p).wait()
        block_copy(out_ref, out_hbm, out_sem, p, 16).wait()


def filter_grad_kernel(
    spec_ref, inner_ref, member_ref, turn_cos_ref, turn_sin_ref, grad_ref, filter_ref, sum_ref
):
    sum_ref[...] = jnp.zeros_like(sum_ref)

    def body(start, count, packed):
        for k in range(count):
            real, imag = apart(spec_ref[start + k].astype(F32))
            both = together(
                *times(
                    real[..., :LANES], imag[..., :LANES], real[..., LANES:], imag[..., LANES:],
                    True, packed,
                )
            )
            high = both.astype(BF16)
            rest = (both - high.astype(F32)).astype(BF16)
            slab = start + k
            member = member_ref[(slab // 2) % 8, pl.ds(LANES * (slab % 2), LANES), :]
            sum_ref[slab // 16] += dot(high, member) + dot(rest, member)

    slabs(body, 4)
    total = jnp.concatenate([sum_ref[0], sum_ref[1]], 1).astype(BF16)
    back = dot(inner_ref[2], total)
    back_zero = dot(inner_ref[3], total)
    packed = lax.broadcasted_iota(jnp.int32, back.shape, 1) < 8
    back = jnp.where(packed, back_zero, back)
    br, bi = back[:INNER], back[INNER:]
    c, s = turn_cos_ref[...], turn_sin_ref[...]
    turned = jnp.concatenate([br * c - bi * s, br * s + bi * c], 1).astype(BF16)
    filter_ref[...] = dot(turned, grad_ref[...]).T


def row_copy(source, target, sem, i, rows):
    cut = pl.ds(i * rows, rows)
    return pltpu.make_async_copy(source.at[cut], target.at[cut], sem.at[i])


def block_copy(source, target, sem, i, rows):
    cut = pl.ds(i * rows, rows)
    return pltpu.make_async_copy(source.at[:, :, cut], target.at[:, :, cut], sem.at[i])


def product(left, right):
    return (left.astype(F32) * right.astype(F32)).astype(BF16)


def gather_kernel(
    gate_hbm, input_hbm, cotan_hbm, out_hbm, gate_ref, input_ref, cotan_ref, out_ref,
    gate_sem, input_sem, cotan_sem, out_sem,
):
    operands = (
        (gate_hbm, gate_ref, gate_sem),
        (cotan_hbm, cotan_ref, cotan_sem),
        (input_hbm, input_ref, input_sem),
    )
    for i in range(CUTS):
        for operand in operands:
            row_copy(*operand, i, CUT).start()
    for i in range(CUTS):
        for operand in operands:
            row_copy(*operand, i, CUT).wait()
        rows = pl.ds(i * CUT, CUT)
        for k in range(OUTER):
            lanes = slice(LANES * k, LANES * k + LANES)
            out_ref[k, 0, rows] = input_ref[rows, lanes]
            out_ref[k, 1, rows] = product(cotan_ref[rows, lanes], gate_ref[rows, lanes])
        block_copy(out_ref, out_hbm, out_sem, i, CUT).start()
    for i in range(CUTS):
        block_copy(out_ref, out_hbm, out_sem, i, CUT).wait()


def spread_kernel(
    back_ref, cotan_ref, gate_hbm, input_hbm, gate_ref, input_ref, gate_sem, input_sem
):
    for i in range(CUTS):
        rows = pl.ds(i * CUT, CUT)
        for k in range(OUTER):
            lanes = slice(LANES * k, LANES * k + LANES)
            gate_ref[rows, lanes] = product(cotan_ref[rows, lanes], back_ref[k, 0, rows])
            input_ref[rows, lanes] = back_ref[k, 1, rows]
        row_copy(gate_ref, gate_hbm, gate_sem, i, CUT).start()
        row_copy(input_ref, input_hbm, input_sem, i, CUT).start()
    for i in range(CUTS):
        row_copy(gate_ref, gate_hbm, gate_sem, i, CUT).wait()
        row_copy(input_ref, input_hbm, input_sem, i, CUT).wait()


CUT = 32
CUTS = INNER // CUT
MOVED = jax.ShapeDtypeStruct((OUTER, 2, INNER, LANES), BF16)
ROWS = jax.ShapeDtypeStruct((INNER, OUTER * LANES), BF16)
HELD = jax.ShapeDtypeStruct((OUTER, PAIR, PAIR), BF16)
IN_HBM = pl.BlockSpec(memory_space=pltpu.HBM)
IN_VMEM = pl.BlockSpec(memory_space=pltpu.VMEM)
DMA = pltpu.SemaphoreType.DMA


def gather(gate, given, cotan):
    return pl.pallas_call(
        gather_kernel,
        out_shape=MOVED,
        in_specs=[IN_HBM] * 3,
        out_specs=IN_HBM,
        scratch_shapes=[pltpu.VMEM(ROWS.shape, BF16)] * 3
        + [pltpu.VMEM(MOVED.shape, BF16)]
        + [DMA((CUTS,))] * 4,
        compiler_params=pltpu.CompilerParams(vmem_limit_bytes=60 << 20),
    )(gate, given, cotan)


def spread(back, cotan):
    return pl.pallas_call(
        spread_kernel,
        out_shape=(ROWS, ROWS),
        in_specs=[IN_VMEM] * 2,
        out_specs=(IN_HBM, IN_HBM),
        scratch_shapes=[pltpu.VMEM(ROWS.shape, BF16)] * 2 + [DMA((CUTS,))] * 2,
        compiler_params=pltpu.CompilerParams(vmem_limit_bytes=8 << 20),
    )(back, cotan)


def call(kernel, operands, outs, scratch, flops, limit):
    space = pl.BlockSpec(memory_space=pltpu.VMEM)
    return pl.pallas_call(
        kernel,
        out_shape=outs,
        in_specs=[space] * len(operands),
        out_specs=jax.tree.map(lambda _: space, outs),
        scratch_shapes=scratch,
        compiler_params=pltpu.CompilerParams(vmem_limit_bytes=limit),
        cost_estimate=pl.CostEstimate(flops=flops, bytes_accessed=16 << 20, transcendentals=0),
    )(*operands)


def filter_spectrum(t, laid):
    return call(
        filter_kernel,
        (laid, t["one"], t["inner"]),
        jax.ShapeDtypeStruct((OUTER, PAIR, LANES), F32),
        [pltpu.VMEM((OUTER, PAIR, LANES), BF16)],
        4 << 30, 24 << 20,
    )


def main_path(t, moved, kernel_spec, gains):
    operands = (kernel_spec, gains, t["one"], t["inner"], t["last"])
    return pl.pallas_call(
        main_kernel,
        out_shape=(MOVED, HELD),
        in_specs=[IN_VMEM] + [IN_HBM] * len(operands),
        out_specs=(IN_HBM, IN_HBM),
        scratch_shapes=[pltpu.VMEM(o.shape, o.dtype) for o in operands]
        + [
            pltpu.VMEM(MOVED.shape, BF16),
            pltpu.VMEM(HELD.shape, BF16),
            pltpu.VMEM(HELD.shape, F32),
            DMA((8,)), DMA, DMA((8,)), DMA, DMA((8,)), DMA((8,)), DMA((8,)),
        ],
        compiler_params=pltpu.CompilerParams(vmem_limit_bytes=59 << 20),
        cost_estimate=pl.CostEstimate(
            flops=6 << 30, bytes_accessed=20 << 20, transcendentals=0
        ),
    )(moved, *operands)


def filter_gradient(t, spec):
    return call(
        filter_grad_kernel,
        (spec, t["inner"], t["member"], t["turn_cos"], t["turn_sin"], t["grad"]),
        jax.ShapeDtypeStruct((PAIR, LANES), F32),
        [pltpu.VMEM((2, PAIR, LANES), F32)],
        2 << 30, 16 << 20,
    )


def lay_filters(filters):
    groups = filters.shape[0]
    member = np.repeat(np.eye(groups), LANES // groups, axis=1)
    return jnp.einsum(
        "gt,gc->tc", filters, jnp.asarray(member, BF16), preferred_element_type=F32
    ).astype(BF16).reshape(OUTER, INNER, LANES)


def exchange(blocks):
    return lax.all_to_all(blocks, "ctx", split_axis=0, concat_axis=0, tiled=True)


def sum_over_sequences(parts):
    count = lax.axis_size("dp")
    place = lax.axis_index("dp")

    def share(owner):
        return lax.dynamic_index_in_dim(parts, owner, 0, keepdims=False)

    total = share(place)
    for hop in range(1, count):
        total = total + lax.ppermute(
            share((place + hop) % count), "dp", [(i, (i + hop) % count) for i in range(count)]
        )
    return total


def unit(moved_input, moved_grad, filters, gains):
    t = build_tables(1.0 / (8192 * 512))
    moved = jnp.stack([moved_input, moved_grad], 1)
    out, spec = main_path(t, moved, filter_spectrum(t, lay_filters(filters)), gains)
    return out[:, 0], out[:, 1], filter_gradient(t, spec)


def on_device(gate_values, conv_input, cotangent, filters, direct_scale):
    replica_count = lax.axis_size("dp")
    grad_scale = 1.0 / (POINTS * math.sqrt(GROUP_WIDTH * replica_count * POINTS // 2))
    t = build_tables(grad_scale)
    moved = exchange(gather(gate_values[0], conv_input[0], cotangent[0]))
    kernel_spec = filter_spectrum(t, lay_filters(filters))
    out, spec = main_path(t, moved, kernel_spec, direct_scale[None, :])
    back = exchange(out)
    filter_part = filter_gradient(t, spec)
    filter_grad = sum_over_sequences(filter_part.reshape(replica_count, -1, LANES))
    filter_grad = filter_grad.reshape(filters.shape[0], -1)
    gate_grad, input_grad = spread(back, cotangent[0])
    return gate_grad[None], input_grad[None], filter_grad


def solution(mesh):
    placed = (
        P("dp", "ctx", None),
        P("dp", "ctx", None),
        P("dp", "ctx", None),
        P("ctx", None),
        P("ctx"),
    )
    return jax.shard_map(
        on_device,
        mesh=mesh,
        in_specs=placed,
        out_specs=(P("dp", "ctx", None), P("dp", "ctx", None), P("ctx", "dp")),
        check_vma=False,
    )
```

```python
import math

import jax
import jax.numpy as jnp
import numpy as np
from jax import lax
from jax.experimental import pallas as pl
from jax.experimental.pallas import tpu as pltpu
from jax.sharding import PartitionSpec as P

GROUP_WIDTH = 16
OUTER = 32
INNER = 128
POINTS = 8192
LANES = 128
PAIR = 2 * LANES
F32 = jnp.float32
BF16 = jnp.bfloat16


def turns(numerator, denominator):
    angle = 2.0 * np.pi * (np.asarray(numerator) % denominator) / denominator
    return np.cos(angle), np.sin(angle)


def build_tables(grad_scale):
    eye = np.eye(8)
    slab = np.arange(OUTER)[:, None, None]
    outer = np.arange(OUTER)[None, :, None]
    step = np.arange(INNER)[None, None, :]
    cos_part, sin_part = turns(slab * (128 * outer + step), POINTS)
    first = np.concatenate([cos_part, -sin_part], 0)
    first[0] = 1.0
    first[OUTER] = (1.0 - 2.0 * (np.arange(OUTER) % 2))[:, None]
    table_last = np.einsum("rnqs,st->qntrs", first.reshape(64, OUTER, 16, 8), eye)
    table_last = table_last.reshape(16, 256, 512) * (2.0 / POINTS)
    table_one = np.einsum("rn,st->rtns", first[:, :, 0], eye).reshape(512, 256)

    index = np.arange(INNER)
    cos_two, sin_two = turns(index[:, None] * index[None, :], INNER)
    table_three = np.block([[cos_two, -sin_two], [sin_two, cos_two]])
    cos_two, sin_two = turns(
        64 * index[:, None] * index[None, :] + index * np.arange(OUTER)[:, None, None], POINTS
    )
    table_two = np.block([[cos_two, sin_two], [-sin_two, cos_two]])
    half = np.arange(64)
    cos_low, sin_low = turns(half[:, None] * index[None, :], INNER)
    cos_mid, sin_mid = turns((32 + 64 * half[:, None]) * index[None, :], POINTS)
    zero = np.zeros((64, INNER))
    sin_low = -sin_low
    sin_low[0] = 1.0 - 2.0 * (index % 2)
    table_two_zero = np.block(
        [[cos_low, zero], [zero, cos_mid], [sin_low, zero], [zero, -sin_mid]]
    )
    weight = np.ones((256, 1))
    weight[0] = 0.5
    weight[128] = 0.5
    mixed_rows = np.arange(256).reshape(2, 16, 8).transpose(1, 0, 2).reshape(256)
    table_three = table_three[:, mixed_rows]
    table_three_zero = (table_two_zero * weight).T[:, mixed_rows]
    table_two[0] = table_two_zero
    table_two = table_two[:, mixed_rows]

    member = np.zeros((8, 256, LANES))
    for pair in range(8):
        for side in range(2):
            for channel in range(LANES):
                lane = (2 * pair + side) * 8 + channel // GROUP_WIDTH
                member[pair, side * LANES + channel, lane] = 1.0
    slab_lane = np.repeat(np.arange(OUTER), 8)
    group_lane = np.tile(np.arange(8), OUTER)
    turn_cos, turn_sin = turns(index[:, None] * slab_lane[None, :], POINTS)
    last_cos, last_sin = turns(slab_lane[:, None] * np.arange(OUTER)[None, :], 64)
    last_sin = -last_sin
    last_sin[slab_lane == 0] = 1.0 - 2.0 * (np.arange(OUTER) % 2)
    parts = np.stack([last_cos, last_sin])
    same = group_lane[:, None] == np.arange(8)[None, :]
    table_grad = np.einsum("pln,lg->plgn", parts, same)
    table_grad = table_grad.reshape(2, 256, 8, 4, 8).transpose(0, 1, 3, 2, 4)
    table_grad = table_grad.reshape(512, 256) * (2.0 * grad_scale)

    def low(values):
        return jnp.asarray(values, BF16)

    def wide(values):
        return jnp.asarray(values, F32)

    return dict(
        one=low(table_one),
        last=low(table_last),
        two=low(table_two),
        three=low(np.stack([table_three, table_three_zero])),
        member=low(member),
        turn_cos=wide(turn_cos),
        turn_sin=wide(turn_sin),
        grad=low(table_grad),
    )


def dot(left, right):
    return jnp.dot(left, right, preferred_element_type=F32)


def outer_block(given, one_ref, p, u_ref):
    lanes = given.shape[2]
    out = []
    for h in range(2):
        held = given[:, 8 * h : 8 * h + 8].reshape(256, lanes).astype(BF16)
        out.append(dot(one_ref[...], held).reshape(64, 8, lanes))
    both = jnp.concatenate(out, 1).astype(BF16)
    row = p * 16 if isinstance(p, int) else pl.multiple_of(p * 16, 16)
    u_ref[:, pl.ds(row, 16), :] = both[:OUTER]
    u_ref[:, pl.ds(INNER + row, 16), :] = both[OUTER:]


def apart(values):
    values = values.reshape(16, 2, 8, values.shape[1])
    return values[:, 0], values[:, 1]


def together(real, imag):
    return jnp.stack([real, imag], 1).reshape(256, real.shape[2])


def times(ar, ai, br, bi, conjugate, packed):
    cross = ai * bi
    if conjugate:
        real, imag = ar * br + cross, ar * bi - ai * br
    else:
        real, imag = ar * br - cross, ar * bi + ai * br
    if packed:
        place = lax.broadcasted_iota(jnp.int32, ar.shape, 0) * 8
        edge = place + lax.broadcasted_iota(jnp.int32, ar.shape, 1) == 0
        real = jnp.where(edge, ar * br, real)
        imag = jnp.where(edge, cross, imag)
    return real, imag


def lane_cut(values, k, width):
    return values[:, width * k : width * k + width]


def slabs(body, count):
    body(0, 1, True)
    body(1, count - 1, False)

    @pl.loop(1, OUTER // count)
    def _(m):
        body(count * m, count, False)


OUTER_ENDS = (8,)
SLAB_ENDS = (4, 8)
LAST_ENDS = (4, 7, 8)


def groups(ends):
    return [range(start, end) for start, end in zip((0,) + ends[:-1], ends)]


def filter_kernel(v_ref, one_ref, two_ref, spec_ref, u_ref):
    @pl.loop(0, 8)
    def _(p):
        row = pl.multiple_of(p * 16, 16)
        outer_block(v_ref[:, pl.ds(row, 16), :].astype(F32), one_ref, p, u_ref)

    @pl.loop(0, OUTER // 4)
    def _(m):
        for k in range(4):
            spec_ref[4 * m + k] = dot(two_ref[4 * m + k], u_ref[4 * m + k])


def main_kernel(
    v_hbm, gain_hbm, one_hbm, three_hbm, h_hbm, two_hbm, last_hbm, out_hbm, spec_hbm,
    v_ref, gain_ref, one_ref, three_ref, h_ref, two_ref, last_ref, out_ref, u_ref, back_ref,
    v_sem, gain_sem, one_sem, three_sem, h_sem, two_sem, last_sem, out_sem, spec_sem,
):
    def part_copy(source, target, sem, m, size):
        cut = pl.ds(size * m, size)
        return pltpu.make_async_copy(source.at[cut], target.at[cut], sem.at[m])

    def h_copy(m):
        return part_copy(h_hbm, h_ref, h_sem, m, 4)

    def two_copy(m):
        return part_copy(two_hbm, two_ref, two_sem, m, 4)

    def last_copy(p):
        return part_copy(last_hbm, last_ref, last_sem, p, 2)

    def spec_copy(m):
        return part_copy(u_ref, spec_hbm, spec_sem, m, 4)

    def v_copy(p):
        return block_copy(v_hbm, v_ref, v_sem, p, 16)

    one_copy = pltpu.make_async_copy(one_hbm, one_ref, one_sem)
    three_copy = pltpu.make_async_copy(three_hbm, three_ref, three_sem)
    gain_copy = pltpu.make_async_copy(gain_hbm, gain_ref, gain_sem)

    one_copy.start()
    for p in range(8):
        v_copy(p).start()
    three_copy.start()
    gain_copy.start()
    late = [copy(m) for m in range(8) for copy in (two_copy, h_copy)]
    late += [last_copy(p) for p in range(8)]

    one_copy.wait()
    for group in groups(OUTER_ENDS):
        for p in group:
            v_copy(p).wait()
        for p in group:
            for copy in late[2 * p : 2 * p + 2]:
                copy.start()
        for p in group:
            both = v_ref[:, :, pl.ds(16 * p, 16), :].astype(F32)
            outer_block(jnp.concatenate([both[:, 0], both[:, 1]], 2), one_ref, p, u_ref)
    for copy in late[16:]:
        copy.start()
    three_copy.wait()

    def slab(j):
        spec = dot(two_ref[j], u_ref[j])
        real, imag = apart(spec)
        hr, hi = apart(h_ref[j])
        pr, pi = times(hr, hi, real[..., :LANES], imag[..., :LANES], False, j == 0)
        ar, ai = times(hr, hi, real[..., LANES:], imag[..., LANES:], True, j == 0)
        product = together(jnp.concatenate([pr, ar], 2), jnp.concatenate([pi, ai], 2))
        back_ref[j] = dot(three_ref[int(j == 0)], product.astype(BF16))
        u_ref[j] = spec.astype(BF16)

    for group in groups(SLAB_ENDS):
        for m in group:
            two_copy(m).wait()
            h_copy(m).wait()
        for m in group:
            for k in range(4):
                slab(4 * m + k)
        for m in group:
            spec_copy(m).start()
    gain_copy.wait()

    def last_block(p):
        row = p * 16
        gain = gain_ref[...]
        given = v_ref[:, :, pl.ds(row, 16), :].astype(F32)
        out = [[], []]
        for h in range(2):
            held = jnp.concatenate(
                [
                    back_ref[:, pl.ds(INNER * part + row + 8 * h, 8), :].reshape(256, PAIR)
                    for part in range(2)
                ],
                0,
            ).astype(BF16)
            lines = dot(last_ref[2 * p + h], held).reshape(OUTER, 8, PAIR)
            for a in range(2):
                out[a].append(
                    lines[:, :, LANES * a : LANES * a + LANES]
                    + gain * given[:, a, 8 * h : 8 * h + 8]
                )
        for a in range(2):
            out_ref[:, a, pl.ds(row, 16), :] = jnp.concatenate(out[a], 1).astype(BF16)

    for group in groups(LAST_ENDS):
        for p in group:
            last_copy(p).wait()
        for p in group:
            last_block(p)
        for p in group:
            block_copy(out_ref, out_hbm, out_sem, p, 16).start()
    for p in range(8):
        spec_copy(p).wait()
        block_copy(out_ref, out_hbm, out_sem, p, 16).wait()


def filter_grad_kernel(
    spec_ref, three_ref, member_ref, turn_cos_ref, turn_sin_ref, grad_ref, filter_ref, sum_ref
):
    sum_ref[...] = jnp.zeros_like(sum_ref)

    def body(start, count, packed):
        for k in range(count):
            real, imag = apart(spec_ref[start + k].astype(F32))
            both = together(
                *times(
                    real[..., :LANES], imag[..., :LANES], real[..., LANES:], imag[..., LANES:],
                    True, packed,
                )
            )
            high = both.astype(BF16)
            rest = (both - high.astype(F32)).astype(BF16)
            slab = start + k
            member = member_ref[(slab // 2) % 8, pl.ds(LANES * (slab % 2), LANES), :]
            sum_ref[slab // 16] += dot(high, member) + dot(rest, member)

    slabs(body, 4)
    total = jnp.concatenate([sum_ref[0], sum_ref[1]], 1).astype(BF16)
    back = dot(three_ref[0], total)
    back_zero = dot(three_ref[1], total)
    packed = lax.broadcasted_iota(jnp.int32, back.shape, 1) < 8
    back = jnp.where(packed, back_zero, back)
    br, bi = back[:INNER], back[INNER:]
    c, s = turn_cos_ref[...], turn_sin_ref[...]
    turned = jnp.concatenate([br * c - bi * s, br * s + bi * c], 1).astype(BF16)
    filter_ref[...] = dot(turned, grad_ref[...]).T


def row_copy(source, target, sem, i, rows):
    cut = pl.ds(i * rows, rows)
    return pltpu.make_async_copy(source.at[cut], target.at[cut], sem.at[i])


def block_copy(source, target, sem, i, rows):
    cut = pl.ds(i * rows, rows)
    return pltpu.make_async_copy(source.at[:, :, cut], target.at[:, :, cut], sem.at[i])


def product(left, right):
    return (left.astype(F32) * right.astype(F32)).astype(BF16)


def gather_kernel(
    gate_hbm, input_hbm, cotan_hbm, out_hbm, gate_ref, input_ref, cotan_ref, out_ref,
    gate_sem, input_sem, cotan_sem, out_sem,
):
    operands = (
        (gate_hbm, gate_ref, gate_sem),
        (cotan_hbm, cotan_ref, cotan_sem),
        (input_hbm, input_ref, input_sem),
    )
    for i in range(CUTS):
        for operand in operands:
            row_copy(*operand, i, CUT).start()
    for i in range(CUTS):
        for operand in operands:
            row_copy(*operand, i, CUT).wait()
        rows = pl.ds(i * CUT, CUT)
        for k in range(OUTER):
            lanes = slice(LANES * k, LANES * k + LANES)
            out_ref[k, 0, rows] = input_ref[rows, lanes]
            out_ref[k, 1, rows] = product(cotan_ref[rows, lanes], gate_ref[rows, lanes])
        block_copy(out_ref, out_hbm, out_sem, i, CUT).start()
    for i in range(CUTS):
        block_copy(out_ref, out_hbm, out_sem, i, CUT).wait()


def spread_kernel(
    back_ref, cotan_ref, gate_hbm, input_hbm, gate_ref, input_ref, gate_sem, input_sem
):
    for i in range(CUTS):
        rows = pl.ds(i * CUT, CUT)
        for k in range(OUTER):
            lanes = slice(LANES * k, LANES * k + LANES)
            gate_ref[rows, lanes] = product(cotan_ref[rows, lanes], back_ref[k, 0, rows])
            input_ref[rows, lanes] = back_ref[k, 1, rows]
        row_copy(gate_ref, gate_hbm, gate_sem, i, CUT).start()
        row_copy(input_ref, input_hbm, input_sem, i, CUT).start()
    for i in range(CUTS):
        row_copy(gate_ref, gate_hbm, gate_sem, i, CUT).wait()
        row_copy(input_ref, input_hbm, input_sem, i, CUT).wait()


CUT = 32
CUTS = INNER // CUT
MOVED = jax.ShapeDtypeStruct((OUTER, 2, INNER, LANES), BF16)
ROWS = jax.ShapeDtypeStruct((INNER, OUTER * LANES), BF16)
HELD = jax.ShapeDtypeStruct((OUTER, PAIR, PAIR), BF16)
IN_HBM = pl.BlockSpec(memory_space=pltpu.HBM)
IN_VMEM = pl.BlockSpec(memory_space=pltpu.VMEM)
DMA = pltpu.SemaphoreType.DMA


def gather(gate, given, cotan):
    return pl.pallas_call(
        gather_kernel,
        out_shape=MOVED,
        in_specs=[IN_HBM] * 3,
        out_specs=IN_HBM,
        scratch_shapes=[pltpu.VMEM(ROWS.shape, BF16)] * 3
        + [pltpu.VMEM(MOVED.shape, BF16)]
        + [DMA((CUTS,))] * 4,
        compiler_params=pltpu.CompilerParams(vmem_limit_bytes=60 << 20),
    )(gate, given, cotan)


def spread(back, cotan):
    return pl.pallas_call(
        spread_kernel,
        out_shape=(ROWS, ROWS),
        in_specs=[IN_VMEM] * 2,
        out_specs=(IN_HBM, IN_HBM),
        scratch_shapes=[pltpu.VMEM(ROWS.shape, BF16)] * 2 + [DMA((CUTS,))] * 2,
        compiler_params=pltpu.CompilerParams(vmem_limit_bytes=8 << 20),
    )(back, cotan)


def call(kernel, operands, outs, scratch, flops, limit):
    space = pl.BlockSpec(memory_space=pltpu.VMEM)
    return pl.pallas_call(
        kernel,
        out_shape=outs,
        in_specs=[space] * len(operands),
        out_specs=jax.tree.map(lambda _: space, outs),
        scratch_shapes=scratch,
        compiler_params=pltpu.CompilerParams(vmem_limit_bytes=limit),
        cost_estimate=pl.CostEstimate(flops=flops, bytes_accessed=16 << 20, transcendentals=0),
    )(*operands)


def filter_spectrum(t, laid):
    return call(
        filter_kernel,
        (laid, t["one"], t["two"]),
        jax.ShapeDtypeStruct((OUTER, PAIR, LANES), F32),
        [pltpu.VMEM((OUTER, PAIR, LANES), BF16)],
        4 << 30, 24 << 20,
    )


def main_path(t, moved, kernel_spec, gains):
    operands = (moved, gains, t["one"], t["three"], kernel_spec, t["two"], t["last"])
    return pl.pallas_call(
        main_kernel,
        out_shape=(MOVED, HELD),
        in_specs=[IN_HBM] * len(operands),
        out_specs=(IN_HBM, IN_HBM),
        scratch_shapes=[pltpu.VMEM(o.shape, o.dtype) for o in operands]
        + [
            pltpu.VMEM(MOVED.shape, BF16),
            pltpu.VMEM(HELD.shape, BF16),
            pltpu.VMEM(HELD.shape, F32),
            DMA((8,)), DMA, DMA, DMA, DMA((8,)), DMA((8,)), DMA((8,)), DMA((8,)), DMA((8,)),
        ],
        compiler_params=pltpu.CompilerParams(vmem_limit_bytes=60 << 20),
        cost_estimate=pl.CostEstimate(
            flops=6 << 30, bytes_accessed=20 << 20, transcendentals=0
        ),
    )(*operands)


def filter_gradient(t, spec):
    return call(
        filter_grad_kernel,
        (spec, t["three"], t["member"], t["turn_cos"], t["turn_sin"], t["grad"]),
        jax.ShapeDtypeStruct((PAIR, LANES), F32),
        [pltpu.VMEM((2, PAIR, LANES), F32)],
        2 << 30, 60 << 20,
    )


def lay_filters(filters):
    groups = filters.shape[0]
    member = np.repeat(np.eye(groups), LANES // groups, axis=1)
    return jnp.einsum(
        "gt,gc->tc", filters, jnp.asarray(member, BF16), preferred_element_type=F32
    ).astype(BF16).reshape(OUTER, INNER, LANES)


def exchange(blocks):
    return lax.all_to_all(blocks, "ctx", split_axis=0, concat_axis=0, tiled=True)


def sum_over_sequences(parts):
    count = lax.axis_size("dp")
    place = lax.axis_index("dp")

    def share(owner):
        return lax.dynamic_index_in_dim(parts, owner, 0, keepdims=False)

    total = share(place)
    for hop in range(1, count):
        total = total + lax.ppermute(
            share((place + hop) % count), "dp", [(i, (i + hop) % count) for i in range(count)]
        )
    return total


def unit(moved_input, moved_grad, filters, gains):
    t = build_tables(1.0 / (8192 * 512))
    moved = jnp.stack([moved_input, moved_grad], 1)
    out, spec = main_path(t, moved, filter_spectrum(t, lay_filters(filters)), gains)
    return out[:, 0], out[:, 1], filter_gradient(t, spec)


def on_device(gate_values, conv_input, cotangent, filters, direct_scale):
    replica_count = lax.axis_size("dp")
    grad_scale = 1.0 / (POINTS * math.sqrt(GROUP_WIDTH * replica_count * POINTS // 2))
    t = build_tables(grad_scale)
    moved = exchange(gather(gate_values[0], conv_input[0], cotangent[0]))
    kernel_spec = filter_spectrum(t, lay_filters(filters))
    out, spec = main_path(t, moved, kernel_spec, direct_scale[None, :])
    back = exchange(out)
    filter_part = filter_gradient(t, spec)
    filter_grad = sum_over_sequences(filter_part.reshape(replica_count, -1, LANES))
    filter_grad = filter_grad.reshape(filters.shape[0], -1)
    gate_grad, input_grad = spread(back, cotangent[0])
    return gate_grad[None], input_grad[None], filter_grad


def solution(mesh):
    placed = (
        P("dp", "ctx", None),
        P("dp", "ctx", None),
        P("dp", "ctx", None),
        P("ctx", None),
        P("ctx"),
    )
    return jax.shard_map(
        on_device,
        mesh=mesh,
        in_specs=placed,
        out_specs=(P("dp", "ctx", None), P("dp", "ctx", None), P("ctx", "dp")),
        check_vma=False,
    )
```

```python
import math

import jax
import jax.numpy as jnp
import numpy as np
from jax import lax
from jax.experimental import pallas as pl
from jax.experimental.pallas import tpu as pltpu
from jax.sharding import PartitionSpec as P

GROUP_WIDTH = 16
OUTER = 32
INNER = 128
POINTS = 8192
LANES = 128
PAIR = 2 * LANES
F32 = jnp.float32
BF16 = jnp.bfloat16


def turns(numerator, denominator):
    angle = 2.0 * np.pi * (np.asarray(numerator) % denominator) / denominator
    return np.cos(angle), np.sin(angle)


def build_tables(grad_scale):
    eye = np.eye(8)
    slab = np.arange(OUTER)[:, None, None]
    outer = np.arange(OUTER)[None, :, None]
    step = np.arange(INNER)[None, None, :]
    cos_part, sin_part = turns(slab * (128 * outer + step), POINTS)
    first = np.concatenate([cos_part, -sin_part], 0)
    first[0] = 1.0
    first[OUTER] = (1.0 - 2.0 * (np.arange(OUTER) % 2))[:, None]
    table_last = np.einsum("rnqs,st->qntrs", first.reshape(64, OUTER, 16, 8), eye)
    table_last = table_last.reshape(16, 256, 512) * (2.0 / POINTS)
    table_one = np.einsum("rn,st->rtns", first[:, :, 0], eye).reshape(512, 256)

    index = np.arange(INNER)
    cos_two, sin_two = turns(index[:, None] * index[None, :], INNER)
    table_three = np.block([[cos_two, -sin_two], [sin_two, cos_two]])
    cos_two, sin_two = turns(
        64 * index[:, None] * index[None, :] + index * np.arange(OUTER)[:, None, None], POINTS
    )
    table_two = np.block([[cos_two, sin_two], [-sin_two, cos_two]])
    half = np.arange(64)
    cos_low, sin_low = turns(half[:, None] * index[None, :], INNER)
    cos_mid, sin_mid = turns((32 + 64 * half[:, None]) * index[None, :], POINTS)
    zero = np.zeros((64, INNER))
    sin_low = -sin_low
    sin_low[0] = 1.0 - 2.0 * (index % 2)
    table_two_zero = np.block(
        [[cos_low, zero], [zero, cos_mid], [sin_low, zero], [zero, -sin_mid]]
    )
    weight = np.ones((256, 1))
    weight[0] = 0.5
    weight[128] = 0.5
    mixed_rows = np.arange(256).reshape(2, 16, 8).transpose(1, 0, 2).reshape(256)
    table_three = table_three[:, mixed_rows]
    table_three_zero = (table_two_zero * weight).T[:, mixed_rows]
    table_two[0] = table_two_zero
    table_two = table_two[:, mixed_rows]

    member = np.zeros((8, 256, LANES))
    for pair in range(8):
        for side in range(2):
            for channel in range(LANES):
                lane = (2 * pair + side) * 8 + channel // GROUP_WIDTH
                member[pair, side * LANES + channel, lane] = 1.0
    slab_lane = np.repeat(np.arange(OUTER), 8)
    group_lane = np.tile(np.arange(8), OUTER)
    turn_cos, turn_sin = turns(index[:, None] * slab_lane[None, :], POINTS)
    last_cos, last_sin = turns(slab_lane[:, None] * np.arange(OUTER)[None, :], 64)
    last_sin = -last_sin
    last_sin[slab_lane == 0] = 1.0 - 2.0 * (np.arange(OUTER) % 2)
    parts = np.stack([last_cos, last_sin])
    same = group_lane[:, None] == np.arange(8)[None, :]
    table_grad = np.einsum("pln,lg->plgn", parts, same)
    table_grad = table_grad.reshape(2, 256, 8, 4, 8).transpose(0, 1, 3, 4, 2)
    table_grad = table_grad.reshape(512, 256) * (2.0 * grad_scale)

    def low(values):
        return jnp.asarray(values, BF16)

    def wide(values):
        return jnp.asarray(values, F32)

    return dict(
        one=low(table_one),
        last=low(table_last),
        two=low(table_two),
        three=low(np.stack([table_three, table_three_zero])),
        member=low(member),
        turn_cos=wide(turn_cos),
        turn_sin=wide(turn_sin),
        grad=low(table_grad),
    )


def dot(left, right):
    return jnp.dot(left, right, preferred_element_type=F32)


def outer_block(given, one_ref, p, u_ref):
    lanes = given.shape[2]
    out = []
    for h in range(2):
        held = given[:, 8 * h : 8 * h + 8].reshape(256, lanes).astype(BF16)
        out.append(dot(one_ref[...], held).reshape(64, 8, lanes))
    both = jnp.concatenate(out, 1).astype(BF16)
    row = p * 16 if isinstance(p, int) else pl.multiple_of(p * 16, 16)
    u_ref[:, pl.ds(row, 16), :] = both[:OUTER]
    u_ref[:, pl.ds(INNER + row, 16), :] = both[OUTER:]


def apart(values):
    values = values.reshape(16, 2, 8, values.shape[1])
    return values[:, 0], values[:, 1]


def together(real, imag):
    return jnp.stack([real, imag], 1).reshape(256, real.shape[2])


def times(ar, ai, br, bi, conjugate, packed):
    cross = ai * bi
    if conjugate:
        real, imag = ar * br + cross, ar * bi - ai * br
    else:
        real, imag = ar * br - cross, ar * bi + ai * br
    if packed:
        place = lax.broadcasted_iota(jnp.int32, ar.shape, 0) * 8
        edge = place + lax.broadcasted_iota(jnp.int32, ar.shape, 1) == 0
        real = jnp.where(edge, ar * br, real)
        imag = jnp.where(edge, cross, imag)
    return real, imag


def lane_cut(values, k, width):
    return values[:, width * k : width * k + width]


def slabs(body, count):
    body(0, 1, True)
    body(1, count - 1, False)

    @pl.loop(1, OUTER // count)
    def _(m):
        body(count * m, count, False)


OUTER_ENDS = (8,)
SLAB_ENDS = (16,32)
LAST_ENDS = (8,)


def groups(ends):
    return [range(start, end) for start, end in zip((0,) + ends[:-1], ends)]


def filter_kernel(v_ref, one_ref, two_ref, spec_ref, u_ref):
    @pl.loop(0, 8)
    def _(p):
        row = pl.multiple_of(p * 16, 16)
        outer_block(v_ref[:, pl.ds(row, 16), :].astype(F32), one_ref, p, u_ref)

    @pl.loop(0, OUTER // 4)
    def _(m):
        for k in range(4):
            spec_ref[4 * m + k] = dot(two_ref[4 * m + k], u_ref[4 * m + k])


def main_kernel(
    v_hbm, gain_hbm, one_hbm, three_hbm, h_hbm, two_hbm, last_hbm, out_hbm, spec_hbm,
    v_ref, gain_ref, one_ref, three_ref, h_ref, two_ref, last_ref, out_ref, u_ref, back_ref,
    v_sem, gain_sem, one_sem, three_sem, h_sem, two_sem, last_sem, out_sem, spec_sem,
):
    def copies(ends, size, *arrays):
        made = []
        for g, group in enumerate(groups(ends)):
            cut = pl.ds(size * group[0], size * len(group))
            made.append(
                [pltpu.make_async_copy(a.at[cut], b.at[cut], sem.at[g]) for a, b, sem in arrays]
            )
        return made

    def row_copies(ends, source, target, sem):
        made = []
        for g, group in enumerate(groups(ends)):
            cut = pl.ds(16 * group[0], 16 * len(group))
            made.append(
                pltpu.make_async_copy(source.at[:, :, cut], target.at[:, :, cut], sem.at[g])
            )
        return made

    v_copies = row_copies(OUTER_ENDS, v_hbm, v_ref, v_sem)
    slab_copies = copies(SLAB_ENDS, 1, (two_hbm, two_ref, two_sem), (h_hbm, h_ref, h_sem))
    spec_copies = copies(SLAB_ENDS, 1, (u_ref, spec_hbm, spec_sem))
    last_copies = copies(LAST_ENDS, 2, (last_hbm, last_ref, last_sem))
    out_copies = row_copies(LAST_ENDS, out_ref, out_hbm, out_sem)
    one_copy = pltpu.make_async_copy(one_hbm, one_ref, one_sem)
    three_copy = pltpu.make_async_copy(three_hbm, three_ref, three_sem)
    gain_copy = pltpu.make_async_copy(gain_hbm, gain_ref, gain_sem)

    v_copies[0].start()
    one_copy.start()
    for copy in v_copies[1:]:
        copy.start()
    three_copy.start()
    gain_copy.start()

    one_copy.wait()
    for g, group in enumerate(groups(OUTER_ENDS)):
        v_copies[g].wait()
        if g == len(OUTER_ENDS) - 1:
            for copy in sum(slab_copies + last_copies, []):
                copy.start()
        for p in group:
            both = v_ref[:, :, pl.ds(16 * p, 16), :].astype(F32)
            outer_block(jnp.concatenate([both[:, 0], both[:, 1]], 2), one_ref, p, u_ref)
    three_copy.wait()

    def slab(j):
        spec = dot(two_ref[j], u_ref[j])
        real, imag = apart(spec)
        hr, hi = apart(h_ref[j])
        pr, pi = times(hr, hi, real[..., :LANES], imag[..., :LANES], False, j == 0)
        ar, ai = times(hr, hi, real[..., LANES:], imag[..., LANES:], True, j == 0)
        product = together(jnp.concatenate([pr, ar], 2), jnp.concatenate([pi, ai], 2))
        back_ref[j] = dot(three_ref[int(j == 0)], product.astype(BF16))
        u_ref[j] = spec.astype(BF16)

    for g, group in enumerate(groups(SLAB_ENDS)):
        for copy in slab_copies[g]:
            copy.wait()
        for j in group:
            slab(j)
        spec_copies[g][0].start()
    gain_copy.wait()

    def last_block(p):
        row = p * 16
        gain = gain_ref[...]
        given = v_ref[:, :, pl.ds(row, 16), :].astype(F32)
        out = [[], []]
        for h in range(2):
            held = jnp.concatenate(
                [
                    back_ref[:, pl.ds(INNER * part + row + 8 * h, 8), :].reshape(256, PAIR)
                    for part in range(2)
                ],
                0,
            ).astype(BF16)
            lines = dot(last_ref[2 * p + h], held).reshape(OUTER, 8, PAIR)
            for a in range(2):
                out[a].append(
                    lines[:, :, LANES * a : LANES * a + LANES]
                    + gain * given[:, a, 8 * h : 8 * h + 8]
                )
        for a in range(2):
            out_ref[:, a, pl.ds(row, 16), :] = jnp.concatenate(out[a], 1).astype(BF16)

    for copy in sum(last_copies, []):
        copy.wait()
    for g, group in enumerate(groups(LAST_ENDS)):
        for p in group:
            last_block(p)
        out_copies[g].start()
    for copy in sum(spec_copies, []) + out_copies:
        copy.wait()


def filter_grad_kernel(
    spec_ref, three_ref, member_ref, turn_cos_ref, turn_sin_ref, grad_ref, filter_ref, sum_ref
):
    sum_ref[...] = jnp.zeros_like(sum_ref)

    def body(start, count, packed):
        for k in range(count):
            real, imag = apart(spec_ref[start + k].astype(F32))
            both = together(
                *times(
                    real[..., :LANES], imag[..., :LANES], real[..., LANES:], imag[..., LANES:],
                    True, packed,
                )
            )
            high = both.astype(BF16)
            rest = (both - high.astype(F32)).astype(BF16)
            slab = start + k
            member = member_ref[(slab // 2) % 8, pl.ds(LANES * (slab % 2), LANES), :]
            sum_ref[slab // 16] += dot(high, member) + dot(rest, member)

    slabs(body, 4)
    total = jnp.concatenate([sum_ref[0], sum_ref[1]], 1).astype(BF16)
    back = dot(three_ref[0], total)
    back_zero = dot(three_ref[1], total)
    packed = lax.broadcasted_iota(jnp.int32, back.shape, 1) < 8
    back = jnp.where(packed, back_zero, back)
    br, bi = back[:INNER], back[INNER:]
    c, s = turn_cos_ref[...], turn_sin_ref[...]
    turned = jnp.concatenate([br * c - bi * s, br * s + bi * c], 1).astype(BF16)
    rows = dot(turned, grad_ref[...]).T
    for n in range(OUTER):
        lanes = slice(n % 8 * INNER, n % 8 * INNER + INNER)
        filter_ref[n // 8, :, lanes] = rows[8 * n : 8 * n + 8]


def row_copy(source, target, sem, i, rows):
    cut = pl.ds(i * rows, rows)
    return pltpu.make_async_copy(source.at[cut], target.at[cut], sem.at[i])


def block_copy(source, target, sem, i, rows):
    cut = pl.ds(i * rows, rows)
    return pltpu.make_async_copy(source.at[:, :, cut], target.at[:, :, cut], sem.at[i])


def product(left, right):
    return (left.astype(F32) * right.astype(F32)).astype(BF16)


def gather_kernel(
    gate_hbm, input_hbm, cotan_hbm, out_hbm, gate_ref, input_ref, cotan_ref, out_ref,
    gate_sem, input_sem, cotan_sem, out_sem,
):
    operands = (
        (gate_hbm, gate_ref, gate_sem),
        (cotan_hbm, cotan_ref, cotan_sem),
        (input_hbm, input_ref, input_sem),
    )
    for i in range(CUTS):
        for operand in operands:
            row_copy(*operand, i, CUT).start()
    for i in range(CUTS):
        for operand in operands:
            row_copy(*operand, i, CUT).wait()
        rows = pl.ds(i * CUT, CUT)
        for k in range(OUTER):
            lanes = slice(LANES * k, LANES * k + LANES)
            out_ref[k, 0, rows] = input_ref[rows, lanes]
            out_ref[k, 1, rows] = product(cotan_ref[rows, lanes], gate_ref[rows, lanes])
        block_copy(out_ref, out_hbm, out_sem, i, CUT).start()
    for i in range(CUTS):
        block_copy(out_ref, out_hbm, out_sem, i, CUT).wait()


def spread_kernel(
    back_ref, cotan_ref, gate_hbm, input_hbm, gate_ref, input_ref, gate_sem, input_sem
):
    for i in range(CUTS):
        rows = pl.ds(i * CUT, CUT)
        for k in range(OUTER):
            lanes = slice(LANES * k, LANES * k + LANES)
            gate_ref[rows, lanes] = product(cotan_ref[rows, lanes], back_ref[k, 0, rows])
            input_ref[rows, lanes] = back_ref[k, 1, rows]
        row_copy(gate_ref, gate_hbm, gate_sem, i, CUT).start()
        row_copy(input_ref, input_hbm, input_sem, i, CUT).start()
    for i in range(CUTS):
        row_copy(gate_ref, gate_hbm, gate_sem, i, CUT).wait()
        row_copy(input_ref, input_hbm, input_sem, i, CUT).wait()


CUT = 32
CUTS = INNER // CUT
MOVED = jax.ShapeDtypeStruct((OUTER, 2, INNER, LANES), BF16)
ROWS = jax.ShapeDtypeStruct((INNER, OUTER * LANES), BF16)
HELD = jax.ShapeDtypeStruct((OUTER, PAIR, PAIR), BF16)
IN_HBM = pl.BlockSpec(memory_space=pltpu.HBM)
IN_VMEM = pl.BlockSpec(memory_space=pltpu.VMEM)
DMA = pltpu.SemaphoreType.DMA


def gather(gate, given, cotan):
    return pl.pallas_call(
        gather_kernel,
        out_shape=MOVED,
        in_specs=[IN_HBM] * 3,
        out_specs=IN_HBM,
        scratch_shapes=[pltpu.VMEM(ROWS.shape, BF16)] * 3
        + [pltpu.VMEM(MOVED.shape, BF16)]
        + [DMA((CUTS,))] * 4,
        compiler_params=pltpu.CompilerParams(vmem_limit_bytes=60 << 20),
    )(gate, given, cotan)


def spread(back, cotan):
    return pl.pallas_call(
        spread_kernel,
        out_shape=(ROWS, ROWS),
        in_specs=[IN_VMEM] * 2,
        out_specs=(IN_HBM, IN_HBM),
        scratch_shapes=[pltpu.VMEM(ROWS.shape, BF16)] * 2 + [DMA((CUTS,))] * 2,
        compiler_params=pltpu.CompilerParams(vmem_limit_bytes=8 << 20),
    )(back, cotan)


def call(kernel, operands, outs, scratch, flops, limit):
    space = pl.BlockSpec(memory_space=pltpu.VMEM)
    return pl.pallas_call(
        kernel,
        out_shape=outs,
        in_specs=[space] * len(operands),
        out_specs=jax.tree.map(lambda _: space, outs),
        scratch_shapes=scratch,
        compiler_params=pltpu.CompilerParams(vmem_limit_bytes=limit),
        cost_estimate=pl.CostEstimate(flops=flops, bytes_accessed=16 << 20, transcendentals=0),
    )(*operands)


def filter_spectrum(t, laid):
    return call(
        filter_kernel,
        (laid, t["one"], t["two"]),
        jax.ShapeDtypeStruct((OUTER, PAIR, LANES), F32),
        [pltpu.VMEM((OUTER, PAIR, LANES), BF16)],
        4 << 30, 24 << 20,
    )


def main_path(t, moved, kernel_spec, gains):
    operands = (moved, gains, t["one"], t["three"], kernel_spec, t["two"], t["last"])
    return pl.pallas_call(
        main_kernel,
        out_shape=(MOVED, HELD),
        in_specs=[IN_HBM] * len(operands),
        out_specs=(IN_HBM, IN_HBM),
        scratch_shapes=[pltpu.VMEM(o.shape, o.dtype) for o in operands]
        + [
            pltpu.VMEM(MOVED.shape, BF16),
            pltpu.VMEM(HELD.shape, BF16),
            pltpu.VMEM(HELD.shape, F32),
            DMA((len(OUTER_ENDS),)), DMA, DMA, DMA, DMA((len(SLAB_ENDS),)),
            DMA((len(SLAB_ENDS),)), DMA((len(LAST_ENDS),)), DMA((len(LAST_ENDS),)),
            DMA((len(SLAB_ENDS),)),
        ],
        compiler_params=pltpu.CompilerParams(vmem_limit_bytes=60 << 20),
        cost_estimate=pl.CostEstimate(
            flops=6 << 30, bytes_accessed=20 << 20, transcendentals=0
        ),
    )(*operands)


def filter_gradient(t, spec):
    return call(
        filter_grad_kernel,
        (spec, t["three"], t["member"], t["turn_cos"], t["turn_sin"], t["grad"]),
        jax.ShapeDtypeStruct((4, 8, 1024), F32),
        [pltpu.VMEM((2, PAIR, LANES), F32)],
        2 << 30, 60 << 20,
    )


def lay_filters(filters):
    groups = filters.shape[0]
    member = np.repeat(np.eye(groups), LANES // groups, axis=1)
    return jnp.einsum(
        "gt,gc->tc", filters, jnp.asarray(member, BF16), preferred_element_type=F32
    ).astype(BF16).reshape(OUTER, INNER, LANES)


def exchange(blocks):
    return lax.all_to_all(blocks, "ctx", split_axis=0, concat_axis=0, tiled=True)


def shares(parts):
    count = lax.axis_size("dp")
    place = lax.axis_index("dp")

    def share(owner):
        return lax.dynamic_index_in_dim(parts, owner, 0, keepdims=False)

    return [share(place)] + [
        lax.ppermute(
            share((place + hop) % count), "dp", [(i, (i + hop) % count) for i in range(count)]
        )
        for hop in range(1, count)
    ]


def unit(moved_input, moved_grad, filters, gains):
    t = build_tables(1.0 / (8192 * 512))
    moved = jnp.stack([moved_input, moved_grad], 1)
    out, spec = main_path(t, moved, filter_spectrum(t, lay_filters(filters)), gains)
    return out[:, 0], out[:, 1], filter_gradient(t, spec)


def on_device(gate_values, conv_input, cotangent, filters, direct_scale):
    replica_count = lax.axis_size("dp")
    grad_scale = 1.0 / (POINTS * math.sqrt(GROUP_WIDTH * replica_count * POINTS // 2))
    t = build_tables(grad_scale)
    moved = exchange(gather(gate_values[0], conv_input[0], cotangent[0]))
    kernel_spec = filter_spectrum(t, lay_filters(filters))
    out, spec = main_path(t, moved, kernel_spec, direct_scale[None, :])
    back = exchange(out)
    filter_part = filter_gradient(t, spec)
    terms = shares(filter_part)
    gate_grad, input_grad = spread(back, cotangent[0])
    gate_grad, input_grad, terms = lax.optimization_barrier((gate_grad, input_grad, terms))
    filter_grad = sum(terms[1:], terms[0])
    return gate_grad[None], input_grad[None], filter_grad


def solution(mesh):
    placed = (
        P("dp", "ctx", None),
        P("dp", "ctx", None),
        P("dp", "ctx", None),
        P("ctx", None),
        P("ctx"),
    )
    return jax.shard_map(
        on_device,
        mesh=mesh,
        in_specs=placed,
        out_specs=(P("dp", "ctx", None), P("dp", "ctx", None), P("ctx", "dp")),
        check_vma=False,
    )
```

```python
import math

import jax
import jax.numpy as jnp
import numpy as np
from jax import lax
from jax.experimental import pallas as pl
from jax.experimental.pallas import tpu as pltpu
from jax.sharding import PartitionSpec as P

GROUP_WIDTH = 16
OUTER = 32
INNER = 128
POINTS = 8192
LANES = 128
PAIR = 2 * LANES
F32 = jnp.float32
BF16 = jnp.bfloat16


def turns(numerator, denominator):
    angle = 2.0 * np.pi * (np.asarray(numerator) % denominator) / denominator
    return np.cos(angle), np.sin(angle)


def build_tables(grad_scale):
    eye = np.eye(8)
    slab = np.arange(OUTER)[:, None, None]
    outer = np.arange(OUTER)[None, :, None]
    step = np.arange(INNER)[None, None, :]
    cos_part, sin_part = turns(slab * (128 * outer + step), POINTS)
    first = np.concatenate([cos_part, -sin_part], 0)
    first[0] = 1.0
    first[OUTER] = (1.0 - 2.0 * (np.arange(OUTER) % 2))[:, None]
    table_last = np.einsum("rnqs,st->qntrs", first.reshape(64, OUTER, 16, 8), eye)
    table_last = table_last.reshape(16, 256, 512) * (2.0 / POINTS)
    table_one = np.einsum("rn,st->rtns", first[:, :, 0], eye).reshape(512, 256)

    index = np.arange(INNER)
    cos_two, sin_two = turns(index[:, None] * index[None, :], INNER)
    table_three = np.block([[cos_two, -sin_two], [sin_two, cos_two]])
    cos_two, sin_two = turns(
        64 * index[:, None] * index[None, :] + index * np.arange(OUTER)[:, None, None], POINTS
    )
    table_two = np.block([[cos_two, sin_two], [-sin_two, cos_two]])
    half = np.arange(64)
    cos_low, sin_low = turns(half[:, None] * index[None, :], INNER)
    cos_mid, sin_mid = turns((32 + 64 * half[:, None]) * index[None, :], POINTS)
    zero = np.zeros((64, INNER))
    sin_low = -sin_low
    sin_low[0] = 1.0 - 2.0 * (index % 2)
    table_two_zero = np.block(
        [[cos_low, zero], [zero, cos_mid], [sin_low, zero], [zero, -sin_mid]]
    )
    weight = np.ones((256, 1))
    weight[0] = 0.5
    weight[128] = 0.5
    mixed_rows = np.arange(256).reshape(2, 16, 8).transpose(1, 0, 2).reshape(256)
    table_three = table_three[:, mixed_rows]
    table_three_zero = (table_two_zero * weight).T[:, mixed_rows]
    table_two[0] = table_two_zero
    table_two = table_two[:, mixed_rows]

    member = np.zeros((8, 256, LANES))
    for pair in range(8):
        for side in range(2):
            for channel in range(LANES):
                lane = (2 * pair + side) * 8 + channel // GROUP_WIDTH
                member[pair, side * LANES + channel, lane] = 1.0
    slab_lane = np.repeat(np.arange(OUTER), 8)
    group_lane = np.tile(np.arange(8), OUTER)
    turn_cos, turn_sin = turns(index[:, None] * slab_lane[None, :], POINTS)
    last_cos, last_sin = turns(slab_lane[:, None] * np.arange(OUTER)[None, :], 64)
    last_sin = -last_sin
    last_sin[slab_lane == 0] = 1.0 - 2.0 * (np.arange(OUTER) % 2)
    parts = np.stack([last_cos, last_sin])
    same = group_lane[:, None] == np.arange(8)[None, :]
    table_grad = np.einsum("pln,lg->plgn", parts, same)
    table_grad = table_grad.reshape(2, 256, 8, 4, 8).transpose(0, 1, 3, 4, 2)
    table_grad = table_grad.reshape(512, 256) * (2.0 * grad_scale)

    def low(values):
        return jnp.asarray(values, BF16)

    def wide(values):
        return jnp.asarray(values, F32)

    return dict(
        one=low(table_one),
        last=low(table_last),
        two=low(table_two),
        three=low(np.stack([table_three, table_three_zero])),
        member=low(member),
        turn_cos=wide(turn_cos),
        turn_sin=wide(turn_sin),
        grad=low(table_grad),
    )


def dot(left, right):
    return jnp.dot(left, right, preferred_element_type=F32)


def outer_block(given, one_ref, p, u_ref):
    lanes = given.shape[2]
    out = []
    for h in range(2):
        held = given[:, 8 * h : 8 * h + 8].reshape(256, lanes).astype(BF16)
        out.append(dot(one_ref[...], held).reshape(64, 8, lanes))
    both = jnp.concatenate(out, 1).astype(BF16)
    row = p * 16 if isinstance(p, int) else pl.multiple_of(p * 16, 16)
    u_ref[:, pl.ds(row, 16), :] = both[:OUTER]
    u_ref[:, pl.ds(INNER + row, 16), :] = both[OUTER:]


def apart(values):
    values = values.reshape(16, 2, 8, values.shape[1])
    return values[:, 0], values[:, 1]


def together(real, imag):
    return jnp.stack([real, imag], 1).reshape(256, real.shape[2])


def times(ar, ai, br, bi, conjugate, packed):
    cross = ai * bi
    if conjugate:
        real, imag = ar * br + cross, ar * bi - ai * br
    else:
        real, imag = ar * br - cross, ar * bi + ai * br
    if packed:
        place = lax.broadcasted_iota(jnp.int32, ar.shape, 0) * 8
        edge = place + lax.broadcasted_iota(jnp.int32, ar.shape, 1) == 0
        real = jnp.where(edge, ar * br, real)
        imag = jnp.where(edge, cross, imag)
    return real, imag


def lane_cut(values, k, width):
    return values[:, width * k : width * k + width]


def slabs(body, count):
    body(0, 1, True)
    body(1, count - 1, False)

    @pl.loop(1, OUTER // count)
    def _(m):
        body(count * m, count, False)


SLAB_ENDS = (16,32)


def groups(ends):
    return [range(start, end) for start, end in zip((0,) + ends[:-1], ends)]


def filter_kernel(v_ref, one_ref, two_ref, spec_ref, u_ref):
    @pl.loop(0, 8)
    def _(p):
        row = pl.multiple_of(p * 16, 16)
        outer_block(v_ref[:, pl.ds(row, 16), :].astype(F32), one_ref, p, u_ref)

    @pl.loop(0, OUTER // 4)
    def _(m):
        for k in range(4):
            spec = dot(two_ref[4 * m + k], u_ref[4 * m + k])
            spec_ref[4 * m + k] = spec.astype(BF16)


def main_kernel(
    v_ref, gain_ref, one_ref, three_ref, h_hbm, two_hbm, last_hbm, out_hbm, spec_hbm,
    h_ref, two_ref, last_ref, out_ref, u_ref, back_ref,
    h_sem, two_sem, last_sem, out_sem, spec_sem,
):
    def copies(ends, size, *arrays):
        made = []
        for g, group in enumerate(groups(ends)):
            cut = pl.ds(size * group[0], size * len(group))
            made.append(
                [pltpu.make_async_copy(a.at[cut], b.at[cut], sem.at[g]) for a, b, sem in arrays]
            )
        return made

    slab_copies = copies(SLAB_ENDS, 1, (two_hbm, two_ref, two_sem), (h_hbm, h_ref, h_sem))
    spec_copies = copies(SLAB_ENDS, 1, (u_ref, spec_hbm, spec_sem))
    last_copies = copies((16,), 1, (last_hbm, last_ref, last_sem))
    out_copy = pltpu.make_async_copy(out_ref, out_hbm, out_sem)
    for copy in sum(slab_copies + last_copies, []):
        copy.start()
    for p in range(8):
        both = v_ref[:, :, pl.ds(16 * p, 16), :].astype(F32)
        outer_block(jnp.concatenate([both[:, 0], both[:, 1]], 2), one_ref, p, u_ref)

    def slab(j):
        spec = dot(two_ref[j], u_ref[j])
        real, imag = apart(spec)
        hr, hi = apart(h_ref[j].astype(F32))
        pr, pi = times(hr, hi, real[..., :LANES], imag[..., :LANES], False, j == 0)
        ar, ai = times(hr, hi, real[..., LANES:], imag[..., LANES:], True, j == 0)
        product = together(jnp.concatenate([pr, ar], 2), jnp.concatenate([pi, ai], 2))
        back_ref[j] = dot(three_ref[int(j == 0)], product.astype(BF16))
        u_ref[j] = spec.astype(BF16)

    for g, group in enumerate(groups(SLAB_ENDS)):
        for copy in slab_copies[g]:
            copy.wait()
        for j in group:
            slab(j)
        spec_copies[g][0].start()

    def last_block(p):
        row = p * 16
        gain = gain_ref[...]
        given = v_ref[:, :, pl.ds(row, 16), :].astype(F32)
        out = [[], []]
        for h in range(2):
            held = jnp.concatenate(
                [
                    back_ref[:, pl.ds(INNER * part + row + 8 * h, 8), :].reshape(256, PAIR)
                    for part in range(2)
                ],
                0,
            ).astype(BF16)
            lines = dot(last_ref[2 * p + h], held).reshape(OUTER, 8, PAIR)
            for a in range(2):
                out[a].append(
                    lines[:, :, LANES * a : LANES * a + LANES]
                    + gain * given[:, a, 8 * h : 8 * h + 8]
                )
        for a in range(2):
            out_ref[:, a, pl.ds(row, 16), :] = jnp.concatenate(out[a], 1).astype(BF16)

    for copy in sum(last_copies, []):
        copy.wait()
    for p in range(8):
        last_block(p)
    out_copy.start()
    for copy in sum(spec_copies, []):
        copy.wait()
    out_copy.wait()


def filter_grad_kernel(
    spec_ref, three_ref, member_ref, turn_cos_ref, turn_sin_ref, grad_ref, filter_ref, sum_ref
):
    sum_ref[...] = jnp.zeros_like(sum_ref)

    def body(start, count, packed):
        for k in range(count):
            real, imag = apart(spec_ref[start + k].astype(F32))
            both = together(
                *times(
                    real[..., :LANES], imag[..., :LANES], real[..., LANES:], imag[..., LANES:],
                    True, packed,
                )
            )
            high = both.astype(BF16)
            rest = (both - high.astype(F32)).astype(BF16)
            slab = start + k
            member = member_ref[(slab // 2) % 8, pl.ds(LANES * (slab % 2), LANES), :]
            sum_ref[slab // 16] += dot(high, member) + dot(rest, member)

    slabs(body, 4)
    total = jnp.concatenate([sum_ref[0], sum_ref[1]], 1).astype(BF16)
    back = dot(three_ref[0], total)
    back_zero = dot(three_ref[1], total)
    packed = lax.broadcasted_iota(jnp.int32, back.shape, 1) < 8
    back = jnp.where(packed, back_zero, back)
    br, bi = back[:INNER], back[INNER:]
    c, s = turn_cos_ref[...], turn_sin_ref[...]
    turned = jnp.concatenate([br * c - bi * s, br * s + bi * c], 1).astype(BF16)
    rows = dot(turned, grad_ref[...]).T
    for n in range(OUTER):
        lanes = slice(n % 8 * INNER, n % 8 * INNER + INNER)
        filter_ref[n // 8, :, lanes] = rows[8 * n : 8 * n + 8]


def row_copy(source, target, sem, i, rows):
    cut = pl.ds(i * rows, rows)
    return pltpu.make_async_copy(source.at[cut], target.at[cut], sem.at[i])


def block_copy(source, target, sem, i, rows):
    cut = pl.ds(i * rows, rows)
    return pltpu.make_async_copy(source.at[:, :, cut], target.at[:, :, cut], sem.at[i])


def product(left, right):
    return (left.astype(F32) * right.astype(F32)).astype(BF16)


def gather_kernel(
    gate_hbm, input_hbm, cotan_hbm, out_hbm, gate_ref, input_ref, cotan_ref, out_ref,
    gate_sem, input_sem, cotan_sem, out_sem,
):
    operands = (
        (gate_hbm, gate_ref, gate_sem),
        (cotan_hbm, cotan_ref, cotan_sem),
        (input_hbm, input_ref, input_sem),
    )
    for i in range(CUTS):
        for operand in operands:
            row_copy(*operand, i, CUT).start()
    for i in range(CUTS):
        for operand in operands:
            row_copy(*operand, i, CUT).wait()
        rows = pl.ds(i * CUT, CUT)
        for k in range(OUTER):
            lanes = slice(LANES * k, LANES * k + LANES)
            out_ref[k, 0, rows] = input_ref[rows, lanes]
            out_ref[k, 1, rows] = product(cotan_ref[rows, lanes], gate_ref[rows, lanes])
        block_copy(out_ref, out_hbm, out_sem, i, CUT).start()
    for i in range(CUTS):
        block_copy(out_ref, out_hbm, out_sem, i, CUT).wait()


def spread_kernel(
    back_ref, cotan_ref, gate_hbm, input_hbm, gate_ref, input_ref, gate_sem, input_sem
):
    for i in range(CUTS):
        rows = pl.ds(i * CUT, CUT)
        for k in range(OUTER):
            lanes = slice(LANES * k, LANES * k + LANES)
            gate_ref[rows, lanes] = product(cotan_ref[rows, lanes], back_ref[k, 0, rows])
            input_ref[rows, lanes] = back_ref[k, 1, rows]
        row_copy(gate_ref, gate_hbm, gate_sem, i, CUT).start()
        row_copy(input_ref, input_hbm, input_sem, i, CUT).start()
    for i in range(CUTS):
        row_copy(gate_ref, gate_hbm, gate_sem, i, CUT).wait()
        row_copy(input_ref, input_hbm, input_sem, i, CUT).wait()


CUT = 32
CUTS = INNER // CUT
MOVED = jax.ShapeDtypeStruct((OUTER, 2, INNER, LANES), BF16)
ROWS = jax.ShapeDtypeStruct((INNER, OUTER * LANES), BF16)
HELD = jax.ShapeDtypeStruct((OUTER, PAIR, PAIR), BF16)
IN_HBM = pl.BlockSpec(memory_space=pltpu.HBM)
IN_VMEM = pl.BlockSpec(memory_space=pltpu.VMEM)
DMA = pltpu.SemaphoreType.DMA


def gather(gate, given, cotan):
    return pl.pallas_call(
        gather_kernel,
        out_shape=MOVED,
        in_specs=[IN_HBM] * 3,
        out_specs=IN_HBM,
        scratch_shapes=[pltpu.VMEM(ROWS.shape, BF16)] * 3
        + [pltpu.VMEM(MOVED.shape, BF16)]
        + [DMA((CUTS,))] * 4,
        compiler_params=pltpu.CompilerParams(vmem_limit_bytes=60 << 20),
    )(gate, given, cotan)


def spread(back, cotan):
    return pl.pallas_call(
        spread_kernel,
        out_shape=(ROWS, ROWS),
        in_specs=[IN_VMEM] * 2,
        out_specs=(IN_HBM, IN_HBM),
        scratch_shapes=[pltpu.VMEM(ROWS.shape, BF16)] * 2 + [DMA((CUTS,))] * 2,
        compiler_params=pltpu.CompilerParams(vmem_limit_bytes=8 << 20),
    )(back, cotan)


def call(kernel, operands, outs, scratch, flops, limit):
    space = pl.BlockSpec(memory_space=pltpu.VMEM)
    return pl.pallas_call(
        kernel,
        out_shape=outs,
        in_specs=[space] * len(operands),
        out_specs=jax.tree.map(lambda _: space, outs),
        scratch_shapes=scratch,
        compiler_params=pltpu.CompilerParams(vmem_limit_bytes=limit),
        cost_estimate=pl.CostEstimate(flops=flops, bytes_accessed=16 << 20, transcendentals=0),
    )(*operands)


def filter_spectrum(t, laid):
    return call(
        filter_kernel,
        (laid, t["one"], t["two"]),
        jax.ShapeDtypeStruct((OUTER, PAIR, LANES), BF16),
        [pltpu.VMEM((OUTER, PAIR, LANES), BF16)],
        4 << 30, 24 << 20,
    )


def main_path(t, moved, kernel_spec, gains):
    near = (moved, gains, t["one"], t["three"])
    far = (kernel_spec, t["two"], t["last"])
    return pl.pallas_call(
        main_kernel,
        out_shape=(MOVED, HELD),
        in_specs=[IN_VMEM] * len(near) + [IN_HBM] * len(far),
        out_specs=(IN_HBM, IN_HBM),
        scratch_shapes=[pltpu.VMEM(o.shape, o.dtype) for o in far]
        + [
            pltpu.VMEM(MOVED.shape, BF16),
            pltpu.VMEM(HELD.shape, BF16),
            pltpu.VMEM(HELD.shape, F32),
            DMA((len(SLAB_ENDS),)), DMA((len(SLAB_ENDS),)), DMA((1,)), DMA,
            DMA((len(SLAB_ENDS),)),
        ],
        compiler_params=pltpu.CompilerParams(vmem_limit_bytes=60 << 20),
        cost_estimate=pl.CostEstimate(
            flops=6 << 30, bytes_accessed=20 << 20, transcendentals=0
        ),
    )(*near, *far)


def filter_gradient(t, spec):
    return call(
        filter_grad_kernel,
        (spec, t["three"], t["member"], t["turn_cos"], t["turn_sin"], t["grad"]),
        jax.ShapeDtypeStruct((4, 8, 1024), F32),
        [pltpu.VMEM((2, PAIR, LANES), F32)],
        2 << 30, 60 << 20,
    )


def lay_filters(filters):
    groups = filters.shape[0]
    member = np.repeat(np.eye(groups), LANES // groups, axis=1)
    return jnp.einsum(
        "gt,gc->tc", filters, jnp.asarray(member, BF16), preferred_element_type=F32
    ).astype(BF16).reshape(OUTER, INNER, LANES)


def exchange(blocks):
    return lax.all_to_all(blocks, "ctx", split_axis=0, concat_axis=0, tiled=True)


def shares(parts):
    count = lax.axis_size("dp")
    place = lax.axis_index("dp")

    def share(owner):
        return lax.dynamic_index_in_dim(parts, owner, 0, keepdims=False)

    return [share(place)] + [
        lax.ppermute(
            share((place + hop) % count), "dp", [(i, (i + hop) % count) for i in range(count)]
        )
        for hop in range(1, count)
    ]


def unit(moved_input, moved_grad, filters, gains):
    t = build_tables(1.0 / (8192 * 512))
    moved = jnp.stack([moved_input, moved_grad], 1)
    out, spec = main_path(t, moved, filter_spectrum(t, lay_filters(filters)), gains)
    return out[:, 0], out[:, 1], filter_gradient(t, spec)


def on_device(gate_values, conv_input, cotangent, filters, direct_scale):
    replica_count = lax.axis_size("dp")
    grad_scale = 1.0 / (POINTS * math.sqrt(GROUP_WIDTH * replica_count * POINTS // 2))
    t = build_tables(grad_scale)
    moved = exchange(gather(gate_values[0], conv_input[0], cotangent[0]))
    kernel_spec = filter_spectrum(t, lay_filters(filters))
    out, spec = main_path(t, moved, kernel_spec, direct_scale[None, :])
    back = exchange(out)
    filter_part = filter_gradient(t, spec)
    terms = shares(filter_part)
    gate_grad, input_grad = spread(back, cotangent[0])
    gate_grad, input_grad, terms = lax.optimization_barrier((gate_grad, input_grad, terms))
    filter_grad = sum(terms[1:], terms[0])
    return gate_grad[None], input_grad[None], filter_grad


def solution(mesh):
    placed = (
        P("dp", "ctx", None),
        P("dp", "ctx", None),
        P("dp", "ctx", None),
        P("ctx", None),
        P("ctx"),
    )
    return jax.shard_map(
        on_device,
        mesh=mesh,
        in_specs=placed,
        out_specs=(P("dp", "ctx", None), P("dp", "ctx", None), P("ctx", "dp")),
        check_vma=False,
    )
```

```python
import math

import jax
import jax.numpy as jnp
import numpy as np
from jax import lax
from jax.experimental import pallas as pl
from jax.experimental.pallas import tpu as pltpu
from jax.sharding import PartitionSpec as P

GROUP_WIDTH = 16
OUTER = 32
INNER = 128
POINTS = 8192
LANES = 128
PAIR = 2 * LANES
F32 = jnp.float32
BF16 = jnp.bfloat16


def turns(numerator, denominator):
    angle = 2.0 * np.pi * (np.asarray(numerator) % denominator) / denominator
    return np.cos(angle), np.sin(angle)


def build_tables(grad_scale):
    eye = np.eye(8)
    slab = np.arange(OUTER)[:, None, None]
    outer = np.arange(OUTER)[None, :, None]
    step = np.arange(INNER)[None, None, :]
    cos_part, sin_part = turns(slab * (128 * outer + step), POINTS)
    first = np.concatenate([cos_part, -sin_part], 0)
    first[0] = 1.0
    first[OUTER] = (1.0 - 2.0 * (np.arange(OUTER) % 2))[:, None]
    table_last = np.einsum("rnqs,st->qntrs", first.reshape(64, OUTER, 16, 8), eye)
    table_last = table_last.reshape(16, 256, 512) * (2.0 / POINTS)
    table_one = np.einsum("rn,st->rtns", first[:, :, 0], eye).reshape(512, 256)

    index = np.arange(INNER)
    cos_two, sin_two = turns(index[:, None] * index[None, :], INNER)
    table_three = np.block([[cos_two, -sin_two], [sin_two, cos_two]])
    cos_two, sin_two = turns(
        64 * index[:, None] * index[None, :] + index * np.arange(OUTER)[:, None, None], POINTS
    )
    table_two = np.block([[cos_two, sin_two], [-sin_two, cos_two]])
    half = np.arange(64)
    cos_low, sin_low = turns(half[:, None] * index[None, :], INNER)
    cos_mid, sin_mid = turns((32 + 64 * half[:, None]) * index[None, :], POINTS)
    zero = np.zeros((64, INNER))
    sin_low = -sin_low
    sin_low[0] = 1.0 - 2.0 * (index % 2)
    table_two_zero = np.block(
        [[cos_low, zero], [zero, cos_mid], [sin_low, zero], [zero, -sin_mid]]
    )
    weight = np.ones((256, 1))
    weight[0] = 0.5
    weight[128] = 0.5
    mixed_rows = np.arange(256).reshape(2, 16, 8).transpose(1, 0, 2).reshape(256)
    table_three = table_three[:, mixed_rows]
    table_three_zero = (table_two_zero * weight).T[:, mixed_rows]
    table_two[0] = table_two_zero
    table_two = table_two[:, mixed_rows]

    member = np.zeros((8, 256, LANES))
    for pair in range(8):
        for side in range(2):
            for channel in range(LANES):
                lane = (2 * pair + side) * 8 + channel // GROUP_WIDTH
                member[pair, side * LANES + channel, lane] = 1.0
    slab_lane = np.repeat(np.arange(OUTER), 8)
    group_lane = np.tile(np.arange(8), OUTER)
    turn_cos, turn_sin = turns(index[:, None] * slab_lane[None, :], POINTS)
    last_cos, last_sin = turns(slab_lane[:, None] * np.arange(OUTER)[None, :], 64)
    last_sin = -last_sin
    last_sin[slab_lane == 0] = 1.0 - 2.0 * (np.arange(OUTER) % 2)
    parts = np.stack([last_cos, last_sin])
    same = group_lane[:, None] == np.arange(8)[None, :]
    table_grad = np.einsum("pln,lg->plgn", parts, same)
    table_grad = table_grad.reshape(2, 256, 8, 4, 8).transpose(0, 1, 3, 4, 2)
    table_grad = table_grad.reshape(512, 256) * (2.0 * grad_scale)

    def low(values):
        return jnp.asarray(values, BF16)

    def wide(values):
        return jnp.asarray(values, F32)

    return dict(
        one=low(table_one),
        last=low(table_last),
        two=low(table_two),
        three=low(np.stack([table_three, table_three_zero])),
        member=low(member),
        turn_cos=wide(turn_cos),
        turn_sin=wide(turn_sin),
        grad=low(table_grad),
    )


def dot(left, right):
    return jnp.dot(left, right, preferred_element_type=F32)


def outer_block(given, one_ref, p, u_ref):
    lanes = given.shape[2]
    out = []
    for h in range(2):
        held = given[:, 8 * h : 8 * h + 8].reshape(256, lanes).astype(BF16)
        out.append(dot(one_ref[...], held).reshape(64, 8, lanes))
    both = jnp.concatenate(out, 1).astype(BF16)
    row = p * 16 if isinstance(p, int) else pl.multiple_of(p * 16, 16)
    u_ref[:, pl.ds(row, 16), :] = both[:OUTER]
    u_ref[:, pl.ds(INNER + row, 16), :] = both[OUTER:]


def apart(values):
    values = values.reshape(16, 2, 8, values.shape[1])
    return values[:, 0], values[:, 1]


def together(real, imag):
    return jnp.stack([real, imag], 1).reshape(256, real.shape[2])


def times(ar, ai, br, bi, conjugate, packed):
    cross = ai * bi
    if conjugate:
        real, imag = ar * br + cross, ar * bi - ai * br
    else:
        real, imag = ar * br - cross, ar * bi + ai * br
    if packed:
        place = lax.broadcasted_iota(jnp.int32, ar.shape, 0) * 8
        edge = place + lax.broadcasted_iota(jnp.int32, ar.shape, 1) == 0
        real = jnp.where(edge, ar * br, real)
        imag = jnp.where(edge, cross, imag)
    return real, imag


def slabs(body, count):
    body(0, 1, True)
    body(1, count - 1, False)

    @pl.loop(1, OUTER // count)
    def _(m):
        body(count * m, count, False)


SLAB_ENDS = (16,32)


def groups(ends):
    return [range(start, end) for start, end in zip((0,) + ends[:-1], ends)]


def filter_kernel(v_ref, one_ref, two_ref, spec_ref, u_ref):
    @pl.loop(0, 8)
    def _(p):
        row = pl.multiple_of(p * 16, 16)
        outer_block(v_ref[:, pl.ds(row, 16), :].astype(F32), one_ref, p, u_ref)

    @pl.loop(0, OUTER // 4)
    def _(m):
        for k in range(4):
            spec = dot(two_ref[4 * m + k], u_ref[4 * m + k])
            spec_ref[4 * m + k] = spec.astype(BF16)


def main_kernel(
    v_ref, gain_ref, one_ref, three_ref, h_hbm, two_hbm, last_hbm, out_hbm, spec_hbm,
    h_ref, two_ref, last_ref, out_ref, u_ref, back_ref,
    h_sem, two_sem, last_sem, out_sem, spec_sem,
):
    def copies(ends, size, *arrays):
        made = []
        for g, group in enumerate(groups(ends)):
            cut = pl.ds(size * group[0], size * len(group))
            made.append(
                [pltpu.make_async_copy(a.at[cut], b.at[cut], sem.at[g]) for a, b, sem in arrays]
            )
        return made

    slab_copies = copies(SLAB_ENDS, 1, (two_hbm, two_ref, two_sem), (h_hbm, h_ref, h_sem))
    spec_copies = copies(SLAB_ENDS, 1, (u_ref, spec_hbm, spec_sem))
    last_copies = copies((16,), 1, (last_hbm, last_ref, last_sem))
    out_copy = pltpu.make_async_copy(out_ref, out_hbm, out_sem)
    for copy in sum(slab_copies + last_copies, []):
        copy.start()
    for p in range(8):
        both = v_ref[:, :, pl.ds(16 * p, 16), :].astype(F32)
        outer_block(jnp.concatenate([both[:, 0], both[:, 1]], 2), one_ref, p, u_ref)

    def slab(j):
        spec = dot(two_ref[j], u_ref[j])
        real, imag = apart(spec)
        hr, hi = apart(h_ref[j].astype(F32))
        pr, pi = times(hr, hi, real[..., :LANES], imag[..., :LANES], False, j == 0)
        ar, ai = times(hr, hi, real[..., LANES:], imag[..., LANES:], True, j == 0)
        product = together(jnp.concatenate([pr, ar], 2), jnp.concatenate([pi, ai], 2))
        back_ref[j] = dot(three_ref[int(j == 0)], product.astype(BF16))
        u_ref[j] = spec.astype(BF16)

    for g, group in enumerate(groups(SLAB_ENDS)):
        for copy in slab_copies[g]:
            copy.wait()
        for j in group:
            slab(j)
        spec_copies[g][0].start()

    def last_block(p):
        row = p * 16
        gain = gain_ref[...]
        given = v_ref[:, :, pl.ds(row, 16), :].astype(F32)
        out = [[], []]
        for h in range(2):
            held = jnp.concatenate(
                [
                    back_ref[:, pl.ds(INNER * part + row + 8 * h, 8), :].reshape(256, PAIR)
                    for part in range(2)
                ],
                0,
            ).astype(BF16)
            lines = dot(last_ref[2 * p + h], held).reshape(OUTER, 8, PAIR)
            for a in range(2):
                out[a].append(
                    lines[:, :, LANES * a : LANES * a + LANES]
                    + gain * given[:, a, 8 * h : 8 * h + 8]
                )
        for a in range(2):
            out_ref[:, a, pl.ds(row, 16), :] = jnp.concatenate(out[a], 1).astype(BF16)

    for copy in sum(last_copies, []):
        copy.wait()
    for p in range(8):
        last_block(p)
    out_copy.start()
    for copy in sum(spec_copies, []):
        copy.wait()
    out_copy.wait()


def filter_grad_kernel(
    spec_ref, three_ref, member_ref, turn_cos_ref, turn_sin_ref, grad_ref, filter_ref, sum_ref
):
    sum_ref[...] = jnp.zeros_like(sum_ref)

    def body(start, count, packed):
        for k in range(count):
            real, imag = apart(spec_ref[start + k].astype(F32))
            both = together(
                *times(
                    real[..., :LANES], imag[..., :LANES], real[..., LANES:], imag[..., LANES:],
                    True, packed,
                )
            )
            high = both.astype(BF16)
            rest = (both - high.astype(F32)).astype(BF16)
            slab = start + k
            member = member_ref[(slab // 2) % 8, pl.ds(LANES * (slab % 2), LANES), :]
            sum_ref[slab // 16] += dot(high, member) + dot(rest, member)

    slabs(body, 4)
    total = jnp.concatenate([sum_ref[0], sum_ref[1]], 1).astype(BF16)
    back = dot(three_ref[0], total)
    back_zero = dot(three_ref[1], total)
    packed = lax.broadcasted_iota(jnp.int32, back.shape, 1) < 8
    back = jnp.where(packed, back_zero, back)
    br, bi = back[:INNER], back[INNER:]
    c, s = turn_cos_ref[...], turn_sin_ref[...]
    turned = jnp.concatenate([br * c - bi * s, br * s + bi * c], 1).astype(BF16)
    rows = dot(turned, grad_ref[...]).T
    for n in range(OUTER):
        lanes = slice(n % 8 * INNER, n % 8 * INNER + INNER)
        filter_ref[n // 8, :, lanes] = rows[8 * n : 8 * n + 8]


def row_copy(source, target, sem, i, rows):
    cut = pl.ds(i * rows, rows)
    return pltpu.make_async_copy(source.at[cut], target.at[cut], sem.at[i])


def block_copy(source, target, sem, i, rows):
    cut = pl.ds(i * rows, rows)
    return pltpu.make_async_copy(source.at[:, :, cut], target.at[:, :, cut], sem.at[i])


def product(left, right):
    return (left.astype(F32) * right.astype(F32)).astype(BF16)


def gather_kernel(
    gate_hbm, input_hbm, cotan_hbm, out_hbm, gate_ref, input_ref, cotan_ref, out_ref,
    gate_sem, input_sem, cotan_sem, out_sem,
):
    operands = (
        (gate_hbm, gate_ref, gate_sem),
        (cotan_hbm, cotan_ref, cotan_sem),
        (input_hbm, input_ref, input_sem),
    )
    for i in range(CUTS):
        for operand in operands:
            row_copy(*operand, i, CUT).start()
    for i in range(CUTS):
        for operand in operands:
            row_copy(*operand, i, CUT).wait()
        rows = pl.ds(i * CUT, CUT)
        for k in range(OUTER):
            lanes = slice(LANES * k, LANES * k + LANES)
            out_ref[k, 0, rows] = input_ref[rows, lanes]
            out_ref[k, 1, rows] = product(cotan_ref[rows, lanes], gate_ref[rows, lanes])
        block_copy(out_ref, out_hbm, out_sem, i, CUT).start()
    for i in range(CUTS):
        block_copy(out_ref, out_hbm, out_sem, i, CUT).wait()


def spread_kernel(
    back_ref, cotan_ref, gate_hbm, input_hbm, gate_ref, input_ref, gate_sem, input_sem
):
    for i in range(CUTS):
        rows = pl.ds(i * CUT, CUT)
        for k in range(OUTER):
            lanes = slice(LANES * k, LANES * k + LANES)
            gate_ref[rows, lanes] = product(cotan_ref[rows, lanes], back_ref[k, 0, rows])
            input_ref[rows, lanes] = back_ref[k, 1, rows]
        row_copy(gate_ref, gate_hbm, gate_sem, i, CUT).start()
        row_copy(input_ref, input_hbm, input_sem, i, CUT).start()
    for i in range(CUTS):
        row_copy(gate_ref, gate_hbm, gate_sem, i, CUT).wait()
        row_copy(input_ref, input_hbm, input_sem, i, CUT).wait()


CUT = 32
CUTS = INNER // CUT
MOVED = jax.ShapeDtypeStruct((OUTER, 2, INNER, LANES), BF16)
ROWS = jax.ShapeDtypeStruct((INNER, OUTER * LANES), BF16)
HELD = jax.ShapeDtypeStruct((OUTER, PAIR, PAIR), BF16)
IN_HBM = pl.BlockSpec(memory_space=pltpu.HBM)
IN_VMEM = pl.BlockSpec(memory_space=pltpu.VMEM)
DMA = pltpu.SemaphoreType.DMA


def gather(gate, given, cotan):
    return pl.pallas_call(
        gather_kernel,
        out_shape=MOVED,
        in_specs=[IN_HBM] * 3,
        out_specs=IN_HBM,
        scratch_shapes=[pltpu.VMEM(ROWS.shape, BF16)] * 3
        + [pltpu.VMEM(MOVED.shape, BF16)]
        + [DMA((CUTS,))] * 4,
        compiler_params=pltpu.CompilerParams(vmem_limit_bytes=60 << 20),
    )(gate, given, cotan)


def spread(back, cotan):
    return pl.pallas_call(
        spread_kernel,
        out_shape=(ROWS, ROWS),
        in_specs=[IN_VMEM] * 2,
        out_specs=(IN_HBM, IN_HBM),
        scratch_shapes=[pltpu.VMEM(ROWS.shape, BF16)] * 2 + [DMA((CUTS,))] * 2,
        compiler_params=pltpu.CompilerParams(vmem_limit_bytes=8 << 20),
    )(back, cotan)


def call(kernel, operands, outs, scratch, flops, limit):
    space = pl.BlockSpec(memory_space=pltpu.VMEM)
    return pl.pallas_call(
        kernel,
        out_shape=outs,
        in_specs=[space] * len(operands),
        out_specs=jax.tree.map(lambda _: space, outs),
        scratch_shapes=scratch,
        compiler_params=pltpu.CompilerParams(vmem_limit_bytes=limit),
        cost_estimate=pl.CostEstimate(flops=flops, bytes_accessed=16 << 20, transcendentals=0),
    )(*operands)


def filter_spectrum(t, laid):
    return call(
        filter_kernel,
        (laid, t["one"], t["two"]),
        jax.ShapeDtypeStruct((OUTER, PAIR, LANES), BF16),
        [pltpu.VMEM((OUTER, PAIR, LANES), BF16)],
        4 << 30, 24 << 20,
    )


def main_path(t, moved, kernel_spec, gains):
    near = (moved, gains, t["one"], t["three"])
    far = (kernel_spec, t["two"], t["last"])
    return pl.pallas_call(
        main_kernel,
        out_shape=(MOVED, HELD),
        in_specs=[IN_VMEM] * len(near) + [IN_HBM] * len(far),
        out_specs=(IN_HBM, IN_HBM),
        scratch_shapes=[pltpu.VMEM(o.shape, o.dtype) for o in far]
        + [
            pltpu.VMEM(MOVED.shape, BF16),
            pltpu.VMEM(HELD.shape, BF16),
            pltpu.VMEM(HELD.shape, F32),
            DMA((len(SLAB_ENDS),)), DMA((len(SLAB_ENDS),)), DMA((1,)), DMA,
            DMA((len(SLAB_ENDS),)),
        ],
        compiler_params=pltpu.CompilerParams(vmem_limit_bytes=60 << 20),
        cost_estimate=pl.CostEstimate(
            flops=6 << 30, bytes_accessed=20 << 20, transcendentals=0
        ),
    )(*near, *far)


def filter_gradient(t, spec):
    return call(
        filter_grad_kernel,
        (spec, t["three"], t["member"], t["turn_cos"], t["turn_sin"], t["grad"]),
        jax.ShapeDtypeStruct((4, 8, 1024), F32),
        [pltpu.VMEM((2, PAIR, LANES), F32)],
        2 << 30, 60 << 20,
    )


def lay_filters(filters):
    groups = filters.shape[0]
    member = np.repeat(np.eye(groups), LANES // groups, axis=1)
    return jnp.einsum(
        "gt,gc->tc", filters, jnp.asarray(member, BF16), preferred_element_type=F32
    ).astype(BF16).reshape(OUTER, INNER, LANES)


def exchange(blocks):
    return lax.all_to_all(blocks, "ctx", split_axis=0, concat_axis=0, tiled=True)


def shares(parts):
    count = lax.axis_size("dp")
    place = lax.axis_index("dp")

    def share(owner):
        return lax.dynamic_index_in_dim(parts, owner, 0, keepdims=False)

    return [share(place)] + [
        lax.ppermute(
            share((place + hop) % count), "dp", [(i, (i + hop) % count) for i in range(count)]
        )
        for hop in range(1, count)
    ]


def on_device(gate_values, conv_input, cotangent, filters, direct_scale):
    replica_count = lax.axis_size("dp")
    grad_scale = 1.0 / (POINTS * math.sqrt(GROUP_WIDTH * replica_count * POINTS // 2))
    t = build_tables(grad_scale)
    moved = exchange(gather(gate_values[0], conv_input[0], cotangent[0]))
    kernel_spec = filter_spectrum(t, lay_filters(filters))
    out, spec = main_path(t, moved, kernel_spec, direct_scale[None, :])
    back = exchange(out)
    filter_part = filter_gradient(t, spec)
    terms = shares(filter_part)
    gate_grad, input_grad = spread(back, cotangent[0])
    gate_grad, input_grad, terms = lax.optimization_barrier((gate_grad, input_grad, terms))
    filter_grad = sum(terms[1:], terms[0])
    return gate_grad[None], input_grad[None], filter_grad


def solution(mesh):
    placed = (
        P("dp", "ctx", None),
        P("dp", "ctx", None),
        P("dp", "ctx", None),
        P("ctx", None),
        P("ctx"),
    )
    return jax.shard_map(
        on_device,
        mesh=mesh,
        in_specs=placed,
        out_specs=(P("dp", "ctx", None), P("dp", "ctx", None), P("ctx", "dp")),
        check_vma=False,
    )
```

```python
import math

import jax
import jax.numpy as jnp
import numpy as np
from jax import lax
from jax.experimental import pallas as pl
from jax.experimental.pallas import tpu as pltpu
from jax.sharding import PartitionSpec as P

GROUP_WIDTH = 16
OUTER = 32
INNER = 128
POINTS = 8192
LANES = 128
PAIR = 2 * LANES
F32 = jnp.float32
BF16 = jnp.bfloat16


def turns(numerator, denominator):
    angle = 2.0 * np.pi * (np.asarray(numerator) % denominator) / denominator
    return np.cos(angle), np.sin(angle)


def build_tables(grad_scale):
    eye = np.eye(8)
    slab = np.arange(OUTER)[:, None, None]
    outer = np.arange(OUTER)[None, :, None]
    step = np.arange(INNER)[None, None, :]
    cos_part, sin_part = turns(slab * (128 * outer + step), POINTS)
    first = np.concatenate([cos_part, -sin_part], 0)
    first[0] = 1.0
    first[OUTER] = (1.0 - 2.0 * (np.arange(OUTER) % 2))[:, None]
    table_last = np.einsum("rnqs,st->qntrs", first.reshape(64, OUTER, 16, 8), eye)
    table_last = table_last.reshape(16, 256, 512) * (2.0 / POINTS)
    table_one = np.einsum("rn,st->rtns", first[:, :, 0], eye).reshape(512, 256)

    index = np.arange(INNER)
    cos_two, sin_two = turns(index[:, None] * index[None, :], INNER)
    table_three = np.block([[cos_two, -sin_two], [sin_two, cos_two]])
    cos_two, sin_two = turns(
        64 * index[:, None] * index[None, :] + index * np.arange(OUTER)[:, None, None], POINTS
    )
    table_two = np.block([[cos_two, sin_two], [-sin_two, cos_two]])
    half = np.arange(64)
    cos_low, sin_low = turns(half[:, None] * index[None, :], INNER)
    cos_mid, sin_mid = turns((32 + 64 * half[:, None]) * index[None, :], POINTS)
    zero = np.zeros((64, INNER))
    sin_low = -sin_low
    sin_low[0] = 1.0 - 2.0 * (index % 2)
    table_two_zero = np.block(
        [[cos_low, zero], [zero, cos_mid], [sin_low, zero], [zero, -sin_mid]]
    )
    weight = np.ones((256, 1))
    weight[0] = 0.5
    weight[128] = 0.5
    mixed_rows = np.arange(256).reshape(2, 16, 8).transpose(1, 0, 2).reshape(256)
    table_three = table_three[:, mixed_rows]
    table_three_zero = (table_two_zero * weight).T[:, mixed_rows]
    table_two[0] = table_two_zero
    table_two = table_two[:, mixed_rows]

    member = np.zeros((8, 256, LANES))
    for pair in range(8):
        for side in range(2):
            for channel in range(LANES):
                lane = (2 * pair + side) * 8 + channel // GROUP_WIDTH
                member[pair, side * LANES + channel, lane] = 1.0
    slab_lane = np.repeat(np.arange(OUTER), 8)
    group_lane = np.tile(np.arange(8), OUTER)
    turn_cos, turn_sin = turns(index[:, None] * slab_lane[None, :], POINTS)
    last_cos, last_sin = turns(slab_lane[:, None] * np.arange(OUTER)[None, :], 64)
    last_sin = -last_sin
    last_sin[slab_lane == 0] = 1.0 - 2.0 * (np.arange(OUTER) % 2)
    parts = np.stack([last_cos, last_sin])
    same = group_lane[:, None] == np.arange(8)[None, :]
    table_grad = np.einsum("pln,lg->plgn", parts, same)
    table_grad = table_grad.reshape(2, 256, 8, 4, 8).transpose(0, 1, 3, 4, 2)
    table_grad = table_grad.reshape(512, 256) * (2.0 * grad_scale)

    def low(values):
        return jnp.asarray(values, BF16)

    def wide(values):
        return jnp.asarray(values, F32)

    return dict(
        one=low(table_one),
        last=low(table_last),
        two=low(table_two),
        three=low(np.stack([table_three, table_three_zero])),
        member=low(member),
        turn_cos=wide(turn_cos),
        turn_sin=wide(turn_sin),
        grad=low(table_grad),
    )


def dot(left, right):
    return jnp.dot(left, right, preferred_element_type=F32)


def outer_block(given, one_ref, p, u_ref):
    lanes = given.shape[2]
    out = []
    for h in range(2):
        held = given[:, 8 * h : 8 * h + 8].reshape(256, lanes).astype(BF16)
        out.append(dot(one_ref[...], held).reshape(64, 8, lanes))
    both = jnp.concatenate(out, 1).astype(BF16)
    row = p * 16 if isinstance(p, int) else pl.multiple_of(p * 16, 16)
    u_ref[:, pl.ds(row, 16), :] = both[:OUTER]
    u_ref[:, pl.ds(INNER + row, 16), :] = both[OUTER:]


def apart(values):
    values = values.reshape(16, 2, 8, values.shape[1])
    return values[:, 0], values[:, 1]


def together(real, imag):
    return jnp.stack([real, imag], 1).reshape(256, real.shape[2])


def times(ar, ai, br, bi, conjugate, packed):
    cross = ai * bi
    if conjugate:
        real, imag = ar * br + cross, ar * bi - ai * br
    else:
        real, imag = ar * br - cross, ar * bi + ai * br
    if packed:
        place = lax.broadcasted_iota(jnp.int32, ar.shape, 0) * 8
        edge = place + lax.broadcasted_iota(jnp.int32, ar.shape, 1) == 0
        real = jnp.where(edge, ar * br, real)
        imag = jnp.where(edge, cross, imag)
    return real, imag


def lane_cut(values, k, width):
    return values[:, width * k : width * k + width]


def slabs(body, count):
    body(0, 1, True)
    body(1, count - 1, False)

    @pl.loop(1, OUTER // count)
    def _(m):
        body(count * m, count, False)


OUTER_ENDS = (8,)
SLAB_ENDS = (16,32)
LAST_ENDS = (8,)


def groups(ends):
    return [range(start, end) for start, end in zip((0,) + ends[:-1], ends)]


def filter_kernel(v_ref, one_ref, two_ref, spec_ref, u_ref):
    @pl.loop(0, 8)
    def _(p):
        row = pl.multiple_of(p * 16, 16)
        outer_block(v_ref[:, pl.ds(row, 16), :].astype(F32), one_ref, p, u_ref)

    @pl.loop(0, OUTER // 4)
    def _(m):
        for k in range(4):
            spec = dot(two_ref[4 * m + k], u_ref[4 * m + k])
            spec_ref[4 * m + k] = spec.astype(spec_ref.dtype)


def main_kernel(
    v_hbm, gain_hbm, one_hbm, three_hbm, h_hbm, two_hbm, last_hbm, out_hbm, spec_hbm,
    v_ref, gain_ref, one_ref, three_ref, h_ref, two_ref, last_ref, out_ref, u_ref, back_ref,
    v_sem, gain_sem, one_sem, three_sem, h_sem, two_sem, last_sem, out_sem, spec_sem,
):
    def copies(ends, size, *arrays):
        made = []
        for g, group in enumerate(groups(ends)):
            cut = pl.ds(size * group[0], size * len(group))
            made.append(
                [pltpu.make_async_copy(a.at[cut], b.at[cut], sem.at[g]) for a, b, sem in arrays]
            )
        return made

    def row_copies(ends, source, target, sem):
        made = []
        for g, group in enumerate(groups(ends)):
            cut = pl.ds(16 * group[0], 16 * len(group))
            made.append(
                pltpu.make_async_copy(source.at[:, :, cut], target.at[:, :, cut], sem.at[g])
            )
        return made

    v_copies = row_copies(OUTER_ENDS, v_hbm, v_ref, v_sem)
    slab_copies = copies(SLAB_ENDS, 1, (two_hbm, two_ref, two_sem), (h_hbm, h_ref, h_sem))
    spec_copies = copies(SLAB_ENDS, 1, (u_ref, spec_hbm, spec_sem))
    last_copies = copies(LAST_ENDS, 2, (last_hbm, last_ref, last_sem))
    out_copies = row_copies(LAST_ENDS, out_ref, out_hbm, out_sem)
    one_copy = pltpu.make_async_copy(one_hbm, one_ref, one_sem)
    three_copy = pltpu.make_async_copy(three_hbm, three_ref, three_sem)
    gain_copy = pltpu.make_async_copy(gain_hbm, gain_ref, gain_sem)

    v_copies[0].start()
    one_copy.start()
    for copy in v_copies[1:]:
        copy.start()
    three_copy.start()
    gain_copy.start()

    for copy in sum(slab_copies + last_copies, []):
        copy.start()
    one_copy.wait()
    for g, group in enumerate(groups(OUTER_ENDS)):
        v_copies[g].wait()
        for p in group:
            both = v_ref[:, :, pl.ds(16 * p, 16), :].astype(F32)
            outer_block(jnp.concatenate([both[:, 0], both[:, 1]], 2), one_ref, p, u_ref)
    three_copy.wait()

    def slab(j):
        spec = dot(two_ref[j], u_ref[j])
        real, imag = apart(spec)
        hr, hi = apart(h_ref[j].astype(F32))
        pr, pi = times(hr, hi, real[..., :LANES], imag[..., :LANES], False, j == 0)
        ar, ai = times(hr, hi, real[..., LANES:], imag[..., LANES:], True, j == 0)
        product = together(jnp.concatenate([pr, ar], 2), jnp.concatenate([pi, ai], 2))
        back_ref[j] = dot(three_ref[int(j == 0)], product.astype(BF16))
        u_ref[j] = spec.astype(BF16)

    for g, group in enumerate(groups(SLAB_ENDS)):
        for copy in slab_copies[g]:
            copy.wait()
        for j in group:
            slab(j)
        spec_copies[g][0].start()
    gain_copy.wait()

    def last_block(p):
        row = p * 16
        gain = gain_ref[...]
        given = v_ref[:, :, pl.ds(row, 16), :].astype(F32)
        out = [[], []]
        for h in range(2):
            held = jnp.concatenate(
                [
                    back_ref[:, pl.ds(INNER * part + row + 8 * h, 8), :].reshape(256, PAIR)
                    for part in range(2)
                ],
                0,
            ).astype(BF16)
            lines = dot(last_ref[2 * p + h], held).reshape(OUTER, 8, PAIR)
            for a in range(2):
                out[a].append(
                    lines[:, :, LANES * a : LANES * a + LANES]
                    + gain * given[:, a, 8 * h : 8 * h + 8]
                )
        for a in range(2):
            out_ref[:, a, pl.ds(row, 16), :] = jnp.concatenate(out[a], 1).astype(BF16)

    for copy in sum(last_copies, []):
        copy.wait()
    for g, group in enumerate(groups(LAST_ENDS)):
        for p in group:
            last_block(p)
        out_copies[g].start()
    for copy in sum(spec_copies, []) + out_copies:
        copy.wait()


def filter_grad_kernel(
    spec_ref, three_ref, member_ref, turn_cos_ref, turn_sin_ref, grad_ref, filter_ref, sum_ref
):
    sum_ref[...] = jnp.zeros_like(sum_ref)

    def body(start, count, packed):
        for k in range(count):
            real, imag = apart(spec_ref[start + k].astype(F32))
            both = together(
                *times(
                    real[..., :LANES], imag[..., :LANES], real[..., LANES:], imag[..., LANES:],
                    True, packed,
                )
            )
            high = both.astype(BF16)
            rest = (both - high.astype(F32)).astype(BF16)
            slab = start + k
            member = member_ref[(slab // 2) % 8, pl.ds(LANES * (slab % 2), LANES), :]
            sum_ref[slab // 16] += dot(high, member) + dot(rest, member)

    slabs(body, 4)
    total = jnp.concatenate([sum_ref[0], sum_ref[1]], 1).astype(BF16)
    back = dot(three_ref[0], total)
    back_zero = dot(three_ref[1], total)
    packed = lax.broadcasted_iota(jnp.int32, back.shape, 1) < 8
    back = jnp.where(packed, back_zero, back)
    br, bi = back[:INNER], back[INNER:]
    c, s = turn_cos_ref[...], turn_sin_ref[...]
    turned = jnp.concatenate([br * c - bi * s, br * s + bi * c], 1).astype(BF16)
    rows = dot(turned, grad_ref[...]).T
    for n in range(OUTER):
        lanes = slice(n % 8 * INNER, n % 8 * INNER + INNER)
        filter_ref[n // 8, :, lanes] = rows[8 * n : 8 * n + 8]


def row_copy(source, target, sem, i, rows):
    cut = pl.ds(i * rows, rows)
    return pltpu.make_async_copy(source.at[cut], target.at[cut], sem.at[i])


def block_copy(source, target, sem, i, rows):
    cut = pl.ds(i * rows, rows)
    return pltpu.make_async_copy(source.at[:, :, cut], target.at[:, :, cut], sem.at[i])


def product(left, right):
    return (left.astype(F32) * right.astype(F32)).astype(BF16)


def gather_kernel(
    gate_hbm, input_hbm, cotan_hbm, out_hbm, gate_ref, input_ref, cotan_ref, out_ref,
    gate_sem, input_sem, cotan_sem, out_sem,
):
    operands = (
        (gate_hbm, gate_ref, gate_sem),
        (cotan_hbm, cotan_ref, cotan_sem),
        (input_hbm, input_ref, input_sem),
    )
    for i in range(CUTS):
        for operand in operands:
            row_copy(*operand, i, CUT).start()
    for i in range(CUTS):
        for operand in operands:
            row_copy(*operand, i, CUT).wait()
        rows = pl.ds(i * CUT, CUT)
        for k in range(OUTER):
            lanes = slice(LANES * k, LANES * k + LANES)
            out_ref[k, 0, rows] = input_ref[rows, lanes]
            out_ref[k, 1, rows] = product(cotan_ref[rows, lanes], gate_ref[rows, lanes])
        block_copy(out_ref, out_hbm, out_sem, i, CUT).start()
    for i in range(CUTS):
        block_copy(out_ref, out_hbm, out_sem, i, CUT).wait()


def spread_kernel(
    back_ref, cotan_ref, gate_hbm, input_hbm, gate_ref, input_ref, gate_sem, input_sem
):
    for i in range(CUTS):
        rows = pl.ds(i * CUT, CUT)
        for k in range(OUTER):
            lanes = slice(LANES * k, LANES * k + LANES)
            gate_ref[rows, lanes] = product(cotan_ref[rows, lanes], back_ref[k, 0, rows])
            input_ref[rows, lanes] = back_ref[k, 1, rows]
        row_copy(gate_ref, gate_hbm, gate_sem, i, CUT).start()
        row_copy(input_ref, input_hbm, input_sem, i, CUT).start()
    for i in range(CUTS):
        row_copy(gate_ref, gate_hbm, gate_sem, i, CUT).wait()
        row_copy(input_ref, input_hbm, input_sem, i, CUT).wait()


CUT = 32
CUTS = INNER // CUT
MOVED = jax.ShapeDtypeStruct((OUTER, 2, INNER, LANES), BF16)
ROWS = jax.ShapeDtypeStruct((INNER, OUTER * LANES), BF16)
HELD = jax.ShapeDtypeStruct((OUTER, PAIR, PAIR), BF16)
IN_HBM = pl.BlockSpec(memory_space=pltpu.HBM)
IN_VMEM = pl.BlockSpec(memory_space=pltpu.VMEM)
DMA = pltpu.SemaphoreType.DMA


def gather(gate, given, cotan):
    return pl.pallas_call(
        gather_kernel,
        out_shape=MOVED,
        in_specs=[IN_HBM] * 3,
        out_specs=IN_HBM,
        scratch_shapes=[pltpu.VMEM(ROWS.shape, BF16)] * 3
        + [pltpu.VMEM(MOVED.shape, BF16)]
        + [DMA((CUTS,))] * 4,
        compiler_params=pltpu.CompilerParams(vmem_limit_bytes=60 << 20),
    )(gate, given, cotan)


def spread(back, cotan):
    return pl.pallas_call(
        spread_kernel,
        out_shape=(ROWS, ROWS),
        in_specs=[IN_VMEM] * 2,
        out_specs=(IN_HBM, IN_HBM),
        scratch_shapes=[pltpu.VMEM(ROWS.shape, BF16)] * 2 + [DMA((CUTS,))] * 2,
        compiler_params=pltpu.CompilerParams(vmem_limit_bytes=8 << 20),
    )(back, cotan)


def call(kernel, operands, outs, scratch, flops, limit):
    space = pl.BlockSpec(memory_space=pltpu.VMEM)
    return pl.pallas_call(
        kernel,
        out_shape=outs,
        in_specs=[space] * len(operands),
        out_specs=jax.tree.map(lambda _: space, outs),
        scratch_shapes=scratch,
        compiler_params=pltpu.CompilerParams(vmem_limit_bytes=limit),
        cost_estimate=pl.CostEstimate(flops=flops, bytes_accessed=16 << 20, transcendentals=0),
    )(*operands)


def filter_spectrum(t, laid):
    return call(
        filter_kernel,
        (laid, t["one"], t["two"]),
        jax.ShapeDtypeStruct((OUTER, PAIR, LANES), BF16),
        [pltpu.VMEM((OUTER, PAIR, LANES), BF16)],
        4 << 30, 24 << 20,
    )


def main_path(t, moved, kernel_spec, gains):
    operands = (moved, gains, t["one"], t["three"], kernel_spec, t["two"], t["last"])
    return pl.pallas_call(
        main_kernel,
        out_shape=(MOVED, HELD),
        in_specs=[IN_HBM] * len(operands),
        out_specs=(IN_HBM, IN_HBM),
        scratch_shapes=[pltpu.VMEM(o.shape, o.dtype) for o in operands]
        + [
            pltpu.VMEM(MOVED.shape, BF16),
            pltpu.VMEM(HELD.shape, BF16),
            pltpu.VMEM(HELD.shape, F32),
            DMA((len(OUTER_ENDS),)), DMA, DMA, DMA, DMA((len(SLAB_ENDS),)),
            DMA((len(SLAB_ENDS),)), DMA((len(LAST_ENDS),)), DMA((len(LAST_ENDS),)),
            DMA((len(SLAB_ENDS),)),
        ],
        compiler_params=pltpu.CompilerParams(vmem_limit_bytes=60 << 20),
        cost_estimate=pl.CostEstimate(
            flops=6 << 30, bytes_accessed=20 << 20, transcendentals=0
        ),
    )(*operands)


def filter_gradient(t, spec):
    return call(
        filter_grad_kernel,
        (spec, t["three"], t["member"], t["turn_cos"], t["turn_sin"], t["grad"]),
        jax.ShapeDtypeStruct((4, 8, 1024), F32),
        [pltpu.VMEM((2, PAIR, LANES), F32)],
        2 << 30, 60 << 20,
    )


def lay_filters(filters):
    groups = filters.shape[0]
    member = np.repeat(np.eye(groups), LANES // groups, axis=1)
    return jnp.einsum(
        "gt,gc->tc", filters, jnp.asarray(member, BF16), preferred_element_type=F32
    ).astype(BF16).reshape(OUTER, INNER, LANES)


def exchange(blocks):
    return lax.all_to_all(blocks, "ctx", split_axis=0, concat_axis=0, tiled=True)


def shares(parts):
    count = lax.axis_size("dp")
    place = lax.axis_index("dp")

    def share(owner):
        return lax.dynamic_index_in_dim(parts, owner, 0, keepdims=False)

    return [share(place)] + [
        lax.ppermute(
            share((place + hop) % count), "dp", [(i, (i + hop) % count) for i in range(count)]
        )
        for hop in range(1, count)
    ]


def on_device(gate_values, conv_input, cotangent, filters, direct_scale):
    replica_count = lax.axis_size("dp")
    grad_scale = 1.0 / (POINTS * math.sqrt(GROUP_WIDTH * replica_count * POINTS // 2))
    t = build_tables(grad_scale)
    moved = exchange(gather(gate_values[0], conv_input[0], cotangent[0]))
    kernel_spec = filter_spectrum(t, lay_filters(filters))
    out, spec = main_path(t, moved, kernel_spec, direct_scale[None, :])
    back = exchange(out)
    filter_part = filter_gradient(t, spec)
    terms = shares(filter_part)
    gate_grad, input_grad = spread(back, cotangent[0])
    gate_grad, input_grad, terms = lax.optimization_barrier((gate_grad, input_grad, terms))
    filter_grad = sum(terms[1:], terms[0])
    return gate_grad[None], input_grad[None], filter_grad


def solution(mesh):
    placed = (
        P("dp", "ctx", None),
        P("dp", "ctx", None),
        P("dp", "ctx", None),
        P("ctx", None),
        P("ctx"),
    )
    return jax.shard_map(
        on_device,
        mesh=mesh,
        in_specs=placed,
        out_specs=(P("dp", "ctx", None), P("dp", "ctx", None), P("ctx", "dp")),
        check_vma=False,
    )
```
